32 devices in a mesh: gx: 16 (over z, y, x), gy: 2 (over core).
Axes of the slice: x: 2, y: 2, z: 4, core: 2. Of those that a mesh axis runs over, the one named last changes fastest.
Arguments:
- adjoint_init: float32 [3, 128, 16, 256], P(None, 'gx', 'gy'), may hold values from -6 to 6
- saved_states: bfloat16 [4, 3, 128, 16, 256], P(None, None, 'gx', 'gy'), may hold values from -4 to 4
- step_index: int32 [4], replicated, may hold values from 0 to 3
- vertical_inverse: float32 [256, 256], replicated, may hold values from -1 to 2
- disk_filter: bfloat16 [16, 2, 8, 64, 512], P('gx', 'gy'), may hold values from -0.25 to 0.25
- pair_turbine: int32 [16, 2, 8], P('gx', 'gy'), may hold values from 0 to 24, as said below
- pair_tile: int32 [16, 2, 8], P('gx', 'gy'), may hold values from 0 to 31
- turbine_owner: int32 [24], replicated, may hold values from 0 to 31
Outputs:
- adjoint_final: float32 [3, 128, 16, 256], P(None, 'gx', 'gy')
- turbine_grad: float32 [16, 2, 24], P('gx', 'gy')
The draws below stay inside these ranges and needn't reach their ends.
Inputs may be any that keep to these rules, and one draw needn't show every extreme that they name: `pair_turbine`: entry 24 marks an empty slot.
All inputs are finite; a program needn't handle non-finite values.
Results may differ from the reference program's by a relative error of at most 0.0024.
Values may be sent and summed in bfloat16 or wider, within the bound.
A program may use at most 64 MiB of HBM per device.

```python
import math
import jax
import jax.numpy as jnp
from jax import lax

CX = 8
CY = 8
NZ = 256
DISK = 64
STEPS = 4
SAVED = 4
SLOTS = 8
TURB_SLAB = 12
TILE = 512
TURB = 24
NDEV = 32
NX = 128
NY = 16
N_GX = 16
N_GY = 2


def draw_vertical_inverse(key, part):
    first_key, second_key = jax.random.split(jax.random.fold_in(key, 11))
    diagonal = jax.random.uniform(first_key, (NZ,), jnp.float32, 0.6, 1.0)
    noise = jax.random.normal(second_key, (NZ, NZ), jnp.float32) / (2.5 * math.sqrt(NZ))
    noise = jnp.clip(noise, -6.0 / (2.5 * math.sqrt(NZ)), 6.0 / (2.5 * math.sqrt(NZ)))
    return (noise + jnp.diag(diagonal)).astype(jnp.float32)


def slab_layout(slab_key):
    first_key, second_key, third_key = jax.random.split(slab_key, 3)
    scores = jax.random.permutation(first_key, N_GX).astype(jnp.int32)
    leading = jax.random.randint(second_key, (), 0, N_GX).astype(jnp.int32)
    follower = (leading + 1) % N_GX
    places = jnp.arange(N_GX, dtype=jnp.int32)
    scores = jnp.where(places == leading, -2, jnp.where(places == follower, -1, scores))
    positions = jnp.argsort(scores, stable=True)[:TURB_SLAB].astype(jnp.int32)
    holder = jnp.full((N_GX,), TURB_SLAB, jnp.int32).at[positions].set(jnp.arange(TURB_SLAB, dtype=jnp.int32))
    spans = jax.random.randint(third_key, (TURB_SLAB,), 0, CY // 2 - 1).astype(jnp.int32)
    spans = spans.at[0].set(CY // 2 - 2)
    return (holder, spans)


def layout_tables(key):
    base = jax.random.fold_in(key, 5)
    slab_keys = jax.random.split(base, N_GY)
    holders, spans = jax.vmap(slab_layout)(slab_keys)
    spans = jnp.concatenate([spans, jnp.zeros((N_GY, 1), jnp.int32)], axis=1)
    left = jnp.transpose(holders)
    right = jnp.roll(left, 1, axis=0)
    slab_ids = jnp.arange(N_GY, dtype=jnp.int32)[None, :]
    half_span = CY // 2
    offsets_x = jnp.array([0, 0, 1, 1], jnp.int32)
    offsets_y = jnp.array([0, 1, 0, 1], jnp.int32)
    left_span = spans[slab_ids, left]
    right_span = spans[slab_ids, right]
    left_tiles = (CX - 2 + offsets_x)[None, None, :] * half_span + left_span[:, :, None] + offsets_y[None, None, :]
    right_tiles = offsets_x[None, None, :] * half_span + right_span[:, :, None] + offsets_y[None, None, :]
    left_live = (left < TURB_SLAB)[:, :, None]
    right_live = (right < TURB_SLAB)[:, :, None]
    left_ids = jnp.where(left_live, slab_ids[:, :, None] * TURB_SLAB + left[:, :, None], TURB) * jnp.ones((1, 1, 4), jnp.int32)
    right_ids = jnp.where(right_live, slab_ids[:, :, None] * TURB_SLAB + right[:, :, None], TURB) * jnp.ones((1, 1, 4), jnp.int32)
    left_tiles = jnp.where(left_live, left_tiles, 0)
    right_tiles = jnp.where(right_live, right_tiles, 0)
    turbine_ids = jnp.concatenate([left_ids, right_ids], axis=2).astype(jnp.int32)
    tile_ids = jnp.concatenate([left_tiles, right_tiles], axis=2).astype(jnp.int32)
    return (turbine_ids, tile_ids)


def draw_pair_turbine(key, part):
    return layout_tables(key)[0]


def draw_pair_tile(key, part):
    return layout_tables(key)[1]


def touch_ends(entries, own_key, least, high):
    place = [jax.random.randint(jax.random.fold_in(own_key, axis), (), 0, length) for axis, length in enumerate(entries.shape)]
    longest = entries.shape.index(max(entries.shape))
    beside = place[:longest] + [(place[longest] + 1) % entries.shape[longest]] + place[longest + 1:]
    return entries.at[tuple(place)].set(least).at[tuple(beside)].set(high)


def level_of(key, extent, shards, low, largest):
    level, own = 1.0, jax.random.fold_in(key, 6)
    for position, shards_of in shards:
        steps = jnp.exp(jax.random.uniform(jax.random.fold_in(own, position), (shards_of,), jnp.float32, low / len(shards), largest / len(shards)))
        level = level * jnp.repeat(steps, extent[position] // shards_of).reshape([-1 if axis == position else 1 for axis in range(len(extent))])
    return level


def scatter_about(rng, shape, scale, most, pieces=(), kind=jnp.bfloat16):
    factor_of = level_of(rng, shape, pieces, -0.22, 0.18) if pieces else 1.0
    entries = jax.random.normal(rng, shape, jnp.float32) * scale * factor_of
    return jnp.minimum(jnp.maximum(entries, -most), most).astype(kind)


def setup_inputs(seed: int = 0) -> dict:
    key_list = jax.random.split(jax.random.key(seed), 9)
    adjoint_init = scatter_about(key_list[0], (3, NX, NY, NZ), 1.0, 6.0, ((1, 16), (2, 2)), jnp.float32)
    saved_states = scatter_about(key_list[1], (SAVED, 3, NX, NY, NZ), 0.7, 4.0, ((2, 16), (3, 2)))
    step_index = touch_ends(jax.random.randint(key_list[2], (STEPS,), 0, SAVED), jax.random.fold_in(key_list[2], 1), 0, SAVED - 1).astype(jnp.int32)
    vertical_inverse = draw_vertical_inverse(jax.random.fold_in(key_list[8], 71), 0)
    disk_filter = scatter_about(key_list[4], (N_GX, N_GY, SLOTS, DISK, TILE), TILE ** -0.5, 0.25, ((0, 16), (1, 2)))
    pair_turbine = draw_pair_turbine(jax.random.fold_in(key_list[8], 71), 0)
    pair_tile = draw_pair_tile(jax.random.fold_in(key_list[8], 71), 0)
    turbine_owner = touch_ends(jax.random.randint(key_list[7], (TURB,), 0, NDEV), jax.random.fold_in(key_list[7], 1), 0, NDEV - 1).astype(jnp.int32)
    return {"adjoint_init": adjoint_init, "saved_states": saved_states, "step_index": step_index, "vertical_inverse": vertical_inverse, "disk_filter": disk_filter, "pair_turbine": pair_turbine, "pair_tile": pair_tile, "turbine_owner": turbine_owner}


COURANT = 0.2


def periodic_difference(values, axis):
    return 0.5 * (jnp.roll(values, -1, axis) - jnp.roll(values, 1, axis))


def vertical_difference(values):
    padded = jnp.pad(values, ((0, 0), (0, 0), (1, 1)))
    return 0.5 * (padded[:, :, 2:] - padded[:, :, :-2])


def reference(adjoint_init, saved_states, step_index, vertical_inverse, disk_filter, pair_turbine, pair_tile, turbine_owner):
    adjoint = adjoint_init
    gradient = jnp.zeros((TURB,), jnp.float32)
    filters = disk_filter.astype(jnp.float32)
    half_span = CY // 2
    stream_index = jnp.arange(N_GX, dtype=jnp.int32)[:, None, None] * CX + pair_tile // half_span
    span_index = jnp.arange(N_GY, dtype=jnp.int32)[None, :, None] * half_span + pair_tile % half_span
    onehot = (pair_turbine[..., None] == jnp.arange(TURB, dtype=jnp.int32)).astype(jnp.float32)
    for number in range(STEPS):
        stored = lax.dynamic_index_in_dim(saved_states, step_index[number].astype(jnp.int32), 0, keepdims=False)
        forward = stored.astype(jnp.float32)
        derivs = [[periodic_difference(forward[source], 0), periodic_difference(forward[source], 1), vertical_difference(forward[source])] for source in range(3)]
        solved = jnp.dot(adjoint.reshape(-1, NZ), vertical_inverse, precision=lax.Precision.HIGHEST, preferred_element_type=jnp.float32).reshape(adjoint.shape)
        updated = []
        for component in range(3):
            current = solved[component]
            advect = forward[0] * periodic_difference(current, 0) + forward[1] * periodic_difference(current, 1) + forward[2] * vertical_difference(current)
            couple = solved[0] * derivs[0][component] + solved[1] * derivs[1][component] + solved[2] * derivs[2][component]
            updated.append(current + COURANT * (advect - couple))
        adjoint = jnp.stack(updated)
        adjoint_tiles = adjoint[0].astype(jnp.bfloat16).reshape(NX, NY // 2, 2 * NZ)
        speed_tiles = stored[0].reshape(NX, NY // 2, 2 * NZ)
        picked_adjoint = adjoint_tiles[stream_index, span_index].astype(jnp.float32)
        picked_speed = speed_tiles[stream_index, span_index].astype(jnp.float32)
        sampled = jnp.einsum("ikjpt,ikjt->ikjp", filters, picked_adjoint, precision=lax.Precision.HIGHEST)
        speeds = jnp.einsum("ikjpt,ikjt->ikjp", filters, picked_speed, precision=lax.Precision.HIGHEST)
        contribs = jnp.mean(speeds * speeds * sampled, axis=-1)
        gradient = gradient + jnp.sum(contribs[..., None] * onehot, axis=(0, 1, 2))
    device_ids = jnp.arange(N_GX, dtype=jnp.int32)[:, None] * N_GY + jnp.arange(N_GY, dtype=jnp.int32)[None, :]
    owned_mask = turbine_owner[None, None, :] == device_ids[:, :, None]
    turbine_grad = jnp.where(owned_mask, gradient[None, None, :], jnp.float32(0.0))
    return adjoint, turbine_grad
```

```python
import functools

import jax
import jax.numpy as jnp
from jax import lax
from jax.experimental import pallas as pl
from jax.experimental.pallas import tpu as pltpu
from jax.sharding import PartitionSpec as P

COURANT = 0.2
HALF = 0.5 * COURANT
MESH = pl.DeviceIdType.MESH
F32 = jnp.float32
BF16 = jnp.bfloat16


def pack(rows):
    parts = [rows[:, k : k + 128] for k in range(0, rows.shape[1], 128)]
    return jnp.concatenate(parts, axis=0).astype(BF16)


def unpack(packed, count):
    wide = packed.astype(F32)
    return jnp.concatenate(
        [wide[k : k + count] for k in range(0, wide.shape[0], count)], axis=1
    )


def read(view, rows):
    return jnp.concatenate([view[k, rows, :] for k in range(view.shape[0])], axis=1)


def write(view, rows, value):
    for k in range(view.shape[0]):
        view[k, rows, :] = value[:, 128 * k : 128 * (k + 1)]


def stream_diff(f):
    zero = jnp.zeros_like(f[:1])
    return jnp.concatenate([f[1:], zero], axis=0) - jnp.concatenate([zero, f[:-1]], axis=0)


def rolled_diff(f, axis):
    size = f.shape[axis]
    place = lax.broadcasted_iota(jnp.int32, f.shape, axis)
    above = jnp.where(place == size - 1, 0.0, pltpu.roll(f, size - 1, axis))
    below = jnp.where(place == 0, 0.0, pltpu.roll(f, 1, axis))
    return above - below


def kernel(
    dims,
    init_hbm, states_hbm, index_hbm, inverse_hbm, filter_hbm, turbine_hbm, tile_hbm, owner_hbm,
    out_hbm, grad_ref,
    adj, states, index_s, inverse, filters, turbine_s, tile_s, owner_s,
    inv_hi, inv_lo, solved, vel, history,
    send_v, recv_v, send_s, recv_s,
    part_y, got_y, part_x, got_x,
    load_sem, out_sem, sv_sem, rv_sem, ss_sem, rs_sem, sy_sem, ry_sem, sx_sem, rx_sem,
):
    ngx, ngy, comps, sx, sy, steps, slots, points, turbines = dims
    cols = sx * sy
    halves = adj.shape[0]
    levels = 128 * halves
    everything = pl.ds(0, comps * cols)
    gx, gy = lax.axis_index("gx"), lax.axis_index("gy")

    loads = [
        pltpu.make_async_copy(src, dst, load_sem.at[k])
        for k, (src, dst) in enumerate((
            (index_hbm, index_s), (states_hbm, states), (inverse_hbm, inverse),
            (turbine_hbm, turbine_s), (tile_hbm, tile_s), (owner_hbm, owner_s), (filter_hbm, filters),
            *((init_hbm.at[:, pl.ds(128 * k, 128)], adj.at[k]) for k in range(halves)),
        ))
    ]
    for load in loads:
        load.start()

    barrier = pltpu.get_barrier_semaphore()

    def greet_x(k, c):
        pl.semaphore_signal(barrier, inc=1, device_id=(lax.rem(gx + k, ngx), gy), device_id_type=MESH)
        return c

    def greet_y(k, c):
        pl.semaphore_signal(barrier, inc=1, device_id=(gx, lax.rem(gy + k, ngy)), device_id_type=MESH)
        return c

    lax.fori_loop(1, ngx, greet_x, 0)
    lax.fori_loop(1, ngy, greet_y, 0)

    beside = (
        (lax.rem(gx + ngx - 1, ngx), gy),
        (lax.rem(gx + 1, ngx), gy),
        (gx, lax.rem(gy + ngy - 1, ngy)),
        (gx, lax.rem(gy + 1, ngy)),
    )

    def edge(c, side):
        base = c * cols
        if side == 0:
            return pl.ds(base, sy)
        if side == 1:
            return pl.ds(base + cols - sy, sy)
        return pl.ds(base + (0 if side == 2 else sy - 1), sx, stride=sy)

    def take(view, c, side):
        return read(view, edge(c, side))

    def put(view, c, side, value):
        write(view, edge(c, side), value)

    def stage(view, staging, s):
        for side in range(4):
            staging[s, side] = pack(
                jnp.concatenate([take(view, c, side) for c in range(comps)], axis=0)
            )

    def copy(staging, landing, ssem, rsem, s, side):
        return pltpu.make_async_remote_copy(
            src_ref=staging.at[s, side],
            dst_ref=landing.at[s, side ^ 1],
            send_sem=ssem.at[s, side],
            recv_sem=rsem.at[s, side ^ 1],
            device_id=beside[side],
            device_id_type=MESH,
        )

    def copies(*refs):
        return [copy(*refs, side) for side in range(4)]

    def prepare(s):
        write(vel.at[s], everything, states[index_s[s]].astype(F32))
        stage(vel.at[s], send_v, s)

    def solve(s):
        value = read(adj, everything)
        hi = value.astype(BF16)
        lo = (value - hi.astype(F32)).astype(BF16)
        dot = functools.partial(jnp.dot, preferred_element_type=F32)
        product = dot(hi, inv_hi[...]) + (dot(hi, inv_lo[...]) + dot(lo, inv_hi[...]))
        write(solved, everything, product)
        stage(solved, send_s, s)

    loads[2].wait()
    whole = inverse[...]
    high = whole.astype(BF16)
    inv_hi[...] = high
    inv_lo[...] = (whole - high.astype(F32)).astype(BF16)
    for load in loads[7:]:
        load.wait()
    solve(0)
    loads[0].wait()
    loads[1].wait()
    prepare(0)

    pl.semaphore_wait(barrier, ngx - 1 + ngy - 1)
    for sent in copies(send_v, recv_v, sv_sem, rv_sem, 0):
        sent.start()

    def step(s, carry):
        for sent in copies(send_s, recv_s, ss_sem, rs_sem, s):
            sent.start()

        @pl.when(s < steps - 1)
        def _():
            prepare(s + 1)
            for sent in copies(send_v, recv_v, sv_sem, rv_sem, s + 1):
                sent.start()

        blocks = lambda view, c: read(view, pl.ds(c * cols, cols)).reshape(sx, sy, levels)
        speed = [blocks(vel.at[s], c) for c in range(comps)]
        differences = (
            stream_diff,
            lambda f: rolled_diff(f, 1),
            lambda f: rolled_diff(f, 2),
        )
        current = [blocks(solved, c) for c in range(comps)]
        for c in range(comps):
            total = 0.0
            for d in range(comps):
                total = total + speed[d] * differences[d](current[c])
                total = total - current[d] * differences[c](speed[d])
            write(adj, pl.ds(c * cols, cols), (current[c] + HALF * total).reshape(cols, levels))

        for side in range(4):
            copy(send_v, recv_v, sv_sem, rv_sem, s, side ^ 1).wait_recv()
            copy(send_s, recv_s, ss_sem, rs_sem, s, side ^ 1).wait_recv()
            sign = -HALF if side % 2 == 0 else HALF
            across = side // 2
            width = sy if across == 0 else sx
            far = unpack(recv_s[s, side], comps * width)
            far_speed = unpack(recv_v[s, side], comps * width)
            carrier = sign * take(vel.at[s], across, side)
            for c in range(comps):
                new = take(adj, c, side) + carrier * far[c * width : (c + 1) * width]
                if c == across:
                    couple = 0.0
                    for d in range(comps):
                        couple = couple + take(solved, d, side) * far_speed[d * width : (d + 1) * width]
                    new = new - sign * couple
                put(adj, c, side, new)

        history[s] = read(adj, pl.ds(0, cols)).astype(BF16)

        @pl.when(s < steps - 1)
        def _():
            solve(s + 1)

        return carry

    lax.fori_loop(0, steps, step, 0)

    outs = [
        pltpu.make_async_copy(adj.at[k], out_hbm.at[:, pl.ds(128 * k, 128)], out_sem.at[k])
        for k in range(halves)
    ]
    for out in outs:
        out.start()

    for load in loads[3:6]:
        load.wait()
    rows = lax.broadcasted_iota(jnp.int32, (2 * slots, cols), 0)
    places = lax.broadcasted_iota(jnp.int32, (2 * slots, cols), 1)
    wanted = jnp.zeros((2 * slots, cols), jnp.int32)
    lanes = got_x.shape[-1]
    slot_rows = lax.broadcasted_iota(jnp.int32, (slots, lanes), 0)
    lane = lax.broadcasted_iota(jnp.int32, (slots, lanes), 1)
    named = jnp.full((slots, lanes), turbines, jnp.int32)
    for j in range(slots):
        first = 2 * tile_s[0, 0, j]
        wanted = jnp.where(rows == j, first, wanted)
        wanted = jnp.where(rows == slots + j, first + 1, wanted)
        named = jnp.where(slot_rows == j, turbine_s[0, 0, j], named)
    pick = jnp.where(wanted == places, 1.0, 0.0).astype(BF16)
    sources = [history[s] for s in range(steps)]
    sources += [read(vel.at[s], pl.ds(0, cols)).astype(BF16) for s in range(steps)]
    vectors = []
    for source in sources:
        picked = jnp.dot(pick, source, preferred_element_type=F32)
        vectors.append(jnp.concatenate([picked[:slots], picked[slots:]], axis=1))
    stacked = jnp.concatenate(vectors, axis=0).astype(BF16)
    loads[6].wait()
    seen = lax.dot_general(
        stacked, filters[...], (((1,), (1,)), ((), ())), preferred_element_type=F32
    )
    terms = 0.0
    for s in range(steps):
        sampled = seen[s * slots : (s + 1) * slots]
        speeds = seen[(steps + s) * slots : (steps + s + 1) * slots]
        terms = terms + speeds * speeds * sampled
    owner_row = lax.broadcasted_iota(jnp.int32, terms.shape, 0)
    owner_col = lax.broadcasted_iota(jnp.int32, terms.shape, 1)
    start = owner_row * points
    inside = (owner_col >= start) & (owner_col < start + points)
    term = jnp.sum(jnp.where(inside, terms, 0.0), axis=1, keepdims=True) * (1.0 / points)
    live = (named == lane) & (lane < turbines)
    part_y[...] = jnp.sum(jnp.where(live, term, 0.0), axis=0, keepdims=True)

    def span_copy(k):
        return pltpu.make_async_remote_copy(
            src_ref=part_y, dst_ref=got_y.at[k - 1],
            send_sem=sy_sem.at[k - 1], recv_sem=ry_sem.at[k - 1],
            device_id=(gx, lax.rem(gy + k, ngy)), device_id_type=MESH,
        )

    def stream_copy(k):
        return pltpu.make_async_remote_copy(
            src_ref=part_x, dst_ref=got_x.at[k - 1],
            send_sem=sx_sem.at[k - 1], recv_sem=rx_sem.at[k - 1],
            device_id=(lax.rem(gx + k, ngx), gy), device_id_type=MESH,
        )

    def run(make, count, act):
        def one(k, c):
            act(make(k))
            return c
        lax.fori_loop(1, count, one, 0)

    run(span_copy, ngy, lambda c: c.start())
    run(span_copy, ngy, lambda c: c.wait_recv())
    part_x[...] = part_y[...] + jnp.sum(got_y[...], axis=0)
    run(stream_copy, ngx, lambda c: c.start())
    mine = jnp.zeros((1, lanes), jnp.int32) - 1
    lane_row = lax.broadcasted_iota(jnp.int32, (1, lanes), 1)
    for t in range(turbines):
        mine = jnp.where(lane_row == t, owner_s[t], mine)
    run(stream_copy, ngx, lambda c: c.wait_recv())
    summed = part_x[...] + jnp.sum(got_x[...], axis=0)
    grad = jnp.where(mine == gx * ngy + gy, summed, 0.0)
    grad_ref[...] = grad[:, :turbines].reshape(grad_ref.shape)

    def drain(s, c):
        for sent in copies(send_v, recv_v, sv_sem, rv_sem, s):
            sent.wait_send()
        for sent in copies(send_s, recv_s, ss_sem, rs_sem, s):
            sent.wait_send()
        return c

    lax.fori_loop(0, steps, drain, 0)
    run(span_copy, ngy, lambda c: c.wait_send())
    run(stream_copy, ngx, lambda c: c.wait_send())
    for out in outs:
        out.wait()


def body(sizes, adjoint_init, saved_states, step_index, vertical_inverse, disk_filter,
         pair_turbine, pair_tile, turbine_owner):
    ngx, ngy = sizes
    comps, sx, sy, levels = adjoint_init.shape
    saved = saved_states.shape[0]
    steps = step_index.shape[0]
    slots, points, cells = disk_filter.shape[2:]
    turbines = turbine_owner.shape[0]
    rows = comps * sx * sy
    lanes = -(-turbines // 128) * 128
    packed = comps * max(sx, sy) * levels // 128
    halves = levels // 128
    dims = (ngx, ngy, comps, sx, sy, steps, slots, points, turbines)
    anywhere = pl.BlockSpec(memory_space=pl.ANY)
    halo = pltpu.VMEM((steps, 4, packed, 128), BF16)
    dma = pltpu.SemaphoreType.DMA
    final, grad = pl.pallas_call(
        functools.partial(kernel, dims),
        out_shape=(
            jax.ShapeDtypeStruct((rows, levels), F32),
            jax.ShapeDtypeStruct((1, 1, turbines), F32),
        ),
        in_specs=[anywhere] * 8,
        out_specs=(anywhere, pl.BlockSpec(memory_space=pltpu.VMEM)),
        scratch_shapes=[
            pltpu.VMEM((halves, rows, 128), F32),
            pltpu.VMEM((saved, rows, levels), BF16),
            pltpu.SMEM(step_index.shape, jnp.int32),
            pltpu.VMEM((levels, levels), F32),
            pltpu.VMEM((slots * points, cells), BF16),
            pltpu.SMEM(pair_turbine.shape, jnp.int32),
            pltpu.SMEM(pair_tile.shape, jnp.int32),
            pltpu.SMEM(turbine_owner.shape, jnp.int32),
            pltpu.VMEM((levels, levels), BF16),
            pltpu.VMEM((levels, levels), BF16),
            pltpu.VMEM((halves, rows, 128), F32),
            pltpu.VMEM((steps, halves, rows, 128), F32),
            pltpu.VMEM((steps, sx * sy, levels), BF16),
            halo, halo, halo, halo,
            pltpu.VMEM((1, lanes), F32),
            pltpu.VMEM((ngy - 1, 1, lanes), F32),
            pltpu.VMEM((1, lanes), F32),
            pltpu.VMEM((ngx - 1, 1, lanes), F32),
            dma((7 + halves,)), dma((halves,)),
            dma((steps, 4)), dma((steps, 4)), dma((steps, 4)), dma((steps, 4)),
            dma((ngy - 1,)), dma((ngy - 1,)), dma((ngx - 1,)), dma((ngx - 1,)),
        ],
        compiler_params=pltpu.CompilerParams(
            collective_id=0, has_side_effects=True, vmem_limit_bytes=48 * 1024 * 1024
        ),
        name="sweep",
    )(
        adjoint_init.reshape(rows, levels),
        saved_states.reshape(saved, rows, levels),
        step_index,
        vertical_inverse,
        disk_filter.reshape(slots * points, cells),
        pair_turbine,
        pair_tile,
        turbine_owner,
    )
    return final.reshape(adjoint_init.shape), grad


def solution(mesh):
    placed = (
        P(None, "gx", "gy", None),
        P(None, None, "gx", "gy", None),
        P(),
        P(),
        P("gx", "gy", None, None, None),
        P("gx", "gy", None),
        P("gx", "gy", None),
        P(),
    )
    return jax.shard_map(
        functools.partial(body, (mesh.shape["gx"], mesh.shape["gy"])),
        mesh=mesh,
        in_specs=placed,
        out_specs=(P(None, "gx", "gy", None), P("gx", "gy", None)),
        check_vma=False,
    )
```

```python
import functools

import jax
import jax.numpy as jnp
from jax import lax
from jax.experimental import pallas as pl
from jax.experimental.pallas import tpu as pltpu
from jax.sharding import PartitionSpec as P

COURANT = 0.2
HALF = 0.5 * COURANT
MESH = pl.DeviceIdType.MESH
F32 = jnp.float32
BF16 = jnp.bfloat16


def pack(rows):
    parts = [rows[:, k : k + 128] for k in range(0, rows.shape[1], 128)]
    return jnp.concatenate(parts, axis=0).astype(BF16)


def unpack(packed, count):
    wide = packed.astype(F32)
    return jnp.concatenate(
        [wide[k : k + count] for k in range(0, wide.shape[0], count)], axis=1
    )


def read(view, rows):
    return jnp.concatenate([view[k, rows, :] for k in range(view.shape[0])], axis=1)


def write(view, rows, value):
    for k in range(view.shape[0]):
        view[k, rows, :] = value[:, 128 * k : 128 * (k + 1)]


def span_diff(tile):
    size = tile.shape[0]
    place = lax.broadcasted_iota(jnp.int32, tile.shape, 0)
    above = jnp.where(place == size - 1, 0.0, pltpu.roll(tile, size - 1, 0))
    below = jnp.where(place == 0, 0.0, pltpu.roll(tile, 1, 0))
    return above - below


def depth_diff(tiles):
    place = lax.broadcasted_iota(jnp.int32, tiles[0].shape, 1)
    ups = [pltpu.roll(tile, 127, 1) for tile in tiles] + [0.0]
    downs = [0.0] + [pltpu.roll(tile, 1, 1) for tile in tiles]
    return [
        jnp.where(place == 127, ups[k + 1], ups[k]) - jnp.where(place == 0, downs[k], downs[k + 1])
        for k in range(len(tiles))
    ]


def kernel(
    dims,
    init_hbm, states_hbm, index_hbm, inverse_hbm, filter_hbm, turbine_hbm, tile_hbm,
    out_hbm, total_ref,
    adj, states, index_s, inverse, filters, turbine_s, tile_s,
    inv_hi, inv_lo, solved, vel, history, pick, weight, terms,
    send_v, recv_v, send_s, recv_s,
    part_y, got_y, part_x, got_x,
    load_sem, out_sem, sv_sem, rv_sem, ss_sem, rs_sem, sy_sem, ry_sem, sx_sem, rx_sem,
):
    ngx, ngy, comps, sx, sy, steps, slots, points, turbines = dims
    cols = sx * sy
    halves = adj.shape[0]
    levels = 128 * halves
    everything = pl.ds(0, comps * cols)
    gx, gy = lax.axis_index("gx"), lax.axis_index("gy")

    loads = [
        pltpu.make_async_copy(src, dst, load_sem.at[k])
        for k, (src, dst) in enumerate((
            (index_hbm, index_s), (states_hbm, states), (inverse_hbm, inverse),
            (turbine_hbm, turbine_s), (tile_hbm, tile_s), (filter_hbm, filters),
            *((init_hbm.at[:, pl.ds(128 * k, 128)], adj.at[k]) for k in range(halves)),
        ))
    ]
    for load in loads:
        load.start()

    barrier = pltpu.get_barrier_semaphore()

    def greet_x(k, c):
        pl.semaphore_signal(barrier, inc=1, device_id=(lax.rem(gx + k, ngx), gy), device_id_type=MESH)
        return c

    def greet_y(k, c):
        pl.semaphore_signal(barrier, inc=1, device_id=(gx, lax.rem(gy + k, ngy)), device_id_type=MESH)
        return c

    lax.fori_loop(1, ngx, greet_x, 0)
    lax.fori_loop(1, ngy, greet_y, 0)

    beside = (
        (lax.rem(gx + ngx - 1, ngx), gy),
        (lax.rem(gx + 1, ngx), gy),
        (gx, lax.rem(gy + ngy - 1, ngy)),
        (gx, lax.rem(gy + 1, ngy)),
    )

    def edge(c, side):
        base = c * cols
        if side == 0:
            return pl.ds(base, sy)
        if side == 1:
            return pl.ds(base + cols - sy, sy)
        return pl.ds(base + (0 if side == 2 else sy - 1), sx, stride=sy)

    def take(view, c, side):
        return read(view, edge(c, side))

    def put(view, c, side, value):
        write(view, edge(c, side), value)

    def stage(view, staging, s, sides):
        for side in sides:
            staging[s, side] = pack(
                jnp.concatenate([take(view, c, side) for c in range(comps)], axis=0)
            )

    def copy(staging, landing, ssem, rsem, s, side):
        return pltpu.make_async_remote_copy(
            src_ref=staging.at[s, side],
            dst_ref=landing.at[s, side ^ 1],
            send_sem=ssem.at[s, side],
            recv_sem=rsem.at[s, side ^ 1],
            device_id=beside[side],
            device_id_type=MESH,
        )

    def copies(*refs):
        return [copy(*refs, side) for side in range(4)]

    def prepare(s):
        write(vel.at[s], everything, states[index_s[s]].astype(F32))
        stage(vel.at[s], send_v, s, range(4))

    def product(value):
        hi = value.astype(BF16)
        lo = (value - hi.astype(F32)).astype(BF16)
        dot = functools.partial(jnp.dot, preferred_element_type=F32)
        return dot(hi, inv_hi[...]) + (dot(hi, inv_lo[...]) + dot(lo, inv_hi[...]))

    def send(staging, landing, ssem, rsem, s, sides):
        for side in sides:
            copy(staging, landing, ssem, rsem, s, side).start()

    def local(s):
        def field(view, c, x):
            if x < 0 or x >= sx:
                return [jnp.zeros((sy, 128), F32)] * halves
            return [view[k, pl.ds(c * cols + x * sy, sy), :] for k in range(halves)]

        def diffs(view, c, x):
            mid = field(view, c, x)
            low, high = field(view, c, x - 1), field(view, c, x + 1)
            return (
                [high[k] - low[k] for k in range(halves)],
                [span_diff(tile) for tile in mid],
                depth_diff(mid),
            )

        speed = vel.at[s]
        for x in range(sx):
            speeds = [field(speed, c, x) for c in range(comps)]
            now = [field(solved, c, x) for c in range(comps)]
            slopes = [diffs(speed, c, x) for c in range(comps)]
            for c in range(comps):
                own = diffs(solved, c, x)
                for k in range(halves):
                    total = speeds[0][k] * own[0][k] - now[0][k] * slopes[0][c][k]
                    for d in range(1, comps):
                        total = total + speeds[d][k] * own[d][k]
                        total = total - now[d][k] * slopes[d][c][k]
                    adj[k, pl.ds(c * cols + x * sy, sy), :] = now[c][k] + HALF * total

    def couple(s, side):
        sign = -HALF if side % 2 == 0 else HALF
        across = side // 2
        width = sy if across == 0 else sx
        far_speed = unpack(recv_v[s, side], comps * width)
        total = take(solved, 0, side) * far_speed[:width]
        for d in range(1, comps):
            total = total + take(solved, d, side) * far_speed[d * width : (d + 1) * width]
        put(adj, across, side, take(adj, across, side) - sign * total)

    def advect(s, side):
        sign = -HALF if side % 2 == 0 else HALF
        across = side // 2
        width = sy if across == 0 else sx
        far = unpack(recv_s[s, side], comps * width)
        carrier = sign * take(vel.at[s], across, side)
        fresh = []
        for c in range(comps):
            new = take(adj, c, side) + carrier * far[c * width : (c + 1) * width]
            put(adj, c, side, new)
            fresh.append(new)
        return fresh

    rows = lax.broadcasted_iota(jnp.int32, (2 * slots, cols), 0)
    places = lax.broadcasted_iota(jnp.int32, (2 * slots, cols), 1)
    lanes = got_x.shape[-1]
    span = slots * points
    slot_row = lax.broadcasted_iota(jnp.int32, (slots, span), 0) * points
    slot_col = lax.broadcasted_iota(jnp.int32, (slots, span), 1)
    inside = (slot_col >= slot_row) & (slot_col < slot_row + points)

    def look(sources):
        vectors = []
        for source in sources:
            found = jnp.dot(pick[...], source, preferred_element_type=F32)
            vectors.append(jnp.concatenate([found[:slots], found[slots:]], axis=1))
        stacked = vectors[0] if len(vectors) == 1 else jnp.concatenate(vectors, axis=0)
        return lax.dot_general(
            stacked.astype(BF16), filters[...], (((1,), (1,)), ((), ())), preferred_element_type=F32
        )

    loads[2].wait()
    whole = inverse[...]
    high = whole.astype(BF16)
    inv_hi[...] = high
    inv_lo[...] = (whole - high.astype(F32)).astype(BF16)
    for load in loads[6:]:
        load.wait()
    write(solved, everything, product(read(adj, everything)))
    stage(solved, send_s, 0, range(4))
    loads[0].wait()
    loads[1].wait()
    prepare(0)

    pl.semaphore_wait(barrier, ngx - 1 + ngy - 1)
    send(send_s, recv_s, ss_sem, rs_sem, 0, range(4))
    send(send_v, recv_v, sv_sem, rv_sem, 0, range(4))

    for load in loads[3:6]:
        load.wait()
    wanted = jnp.zeros((2 * slots, cols), jnp.int32)
    for j in range(slots):
        first = 2 * tile_s[0, 0, j]
        wanted = jnp.where(rows == j, first, wanted)
        wanted = jnp.where(rows == slots + j, first + 1, wanted)
    pick[...] = jnp.where(wanted == places, 1.0, 0.0).astype(BF16)
    history[...] = jnp.zeros_like(history)
    weight[...] = jnp.zeros_like(weight)
    terms[...] = jnp.zeros_like(terms)

    def step(s, carry):
        @pl.when(s < steps - 1)
        def _():
            prepare(s + 1)
            send(send_v, recv_v, sv_sem, rv_sem, s + 1, range(4))

        local(s)
        for side in range(4):
            copy(send_v, recv_v, sv_sem, rv_sem, s, side ^ 1).wait_recv()
            couple(s, side)
        for side in (2, 3):
            copy(send_s, recv_s, ss_sem, rs_sem, s, side ^ 1).wait_recv()
            advect(s, side)

        @pl.when(s < steps - 1)
        def _():
            write(solved, everything, product(read(adj, everything)))

        seen = look((history[...], read(vel.at[s], pl.ds(0, cols)).astype(BF16)))
        terms[...] += weight[...] * seen[:slots]
        speeds = seen[slots:]
        weight[...] = jnp.where(inside, speeds * speeds, 0.0) * (1.0 / points)

        for side in (0, 1):
            copy(send_s, recv_s, ss_sem, rs_sem, s, side ^ 1).wait_recv()
        fresh = advect(s, 0) + advect(s, 1)

        @pl.when(s < steps - 1)
        def _():
            edges = product(jnp.concatenate(fresh, axis=0))
            for side in (0, 1):
                part = edges[side * comps * sy : (side + 1) * comps * sy]
                send_s[s + 1, side] = pack(part)
                send(send_s, recv_s, ss_sem, rs_sem, s + 1, (side,))
                for c in range(comps):
                    put(solved, c, side, part[c * sy : (c + 1) * sy])
            stage(solved, send_s, s + 1, (2, 3))
            send(send_s, recv_s, ss_sem, rs_sem, s + 1, (2, 3))

        history[...] = read(adj, pl.ds(0, cols)).astype(BF16)
        return carry

    lax.fori_loop(0, steps, step, 0)

    outs = [
        pltpu.make_async_copy(adj.at[k], out_hbm.at[:, pl.ds(128 * k, 128)], out_sem.at[k])
        for k in range(halves)
    ]
    for out in outs:
        out.start()

    term = jnp.sum(terms[...] + weight[...] * look((history[...],)), axis=1, keepdims=True)
    slot_rows = lax.broadcasted_iota(jnp.int32, (slots, lanes), 0)
    lane = lax.broadcasted_iota(jnp.int32, (slots, lanes), 1)
    named = jnp.full((slots, lanes), turbines, jnp.int32)
    for j in range(slots):
        named = jnp.where(slot_rows == j, turbine_s[0, 0, j], named)
    live = (named == lane) & (lane < turbines)
    part_y[...] = jnp.sum(jnp.where(live, term, 0.0), axis=0, keepdims=True)

    def span_copy(k):
        return pltpu.make_async_remote_copy(
            src_ref=part_y, dst_ref=got_y.at[k - 1],
            send_sem=sy_sem.at[k - 1], recv_sem=ry_sem.at[k - 1],
            device_id=(gx, lax.rem(gy + k, ngy)), device_id_type=MESH,
        )

    def stream_copy(k):
        return pltpu.make_async_remote_copy(
            src_ref=part_x, dst_ref=got_x.at[k - 1],
            send_sem=sx_sem.at[k - 1], recv_sem=rx_sem.at[k - 1],
            device_id=(lax.rem(gx + k, ngx), gy), device_id_type=MESH,
        )

    def run(make, count, act):
        def one(k, c):
            act(make(k))
            return c
        lax.fori_loop(1, count, one, 0)

    run(span_copy, ngy, lambda c: c.start())
    run(span_copy, ngy, lambda c: c.wait_recv())
    part_x[...] = part_y[...] + jnp.sum(got_y[...], axis=0)
    run(stream_copy, ngx, lambda c: c.start())
    run(stream_copy, ngx, lambda c: c.wait_recv())
    summed = part_x[...] + jnp.sum(got_x[...], axis=0)
    total_ref[...] = summed[:, :turbines].reshape(total_ref.shape)

    def drain(s, c):
        for sent in copies(send_v, recv_v, sv_sem, rv_sem, s):
            sent.wait_send()
        for sent in copies(send_s, recv_s, ss_sem, rs_sem, s):
            sent.wait_send()
        return c

    lax.fori_loop(0, steps, drain, 0)
    run(span_copy, ngy, lambda c: c.wait_send())
    run(stream_copy, ngx, lambda c: c.wait_send())
    for out in outs:
        out.wait()


def body(sizes, adjoint_init, saved_states, step_index, vertical_inverse, disk_filter,
         pair_turbine, pair_tile, turbine_owner):
    ngx, ngy = sizes
    comps, sx, sy, levels = adjoint_init.shape
    saved = saved_states.shape[0]
    steps = step_index.shape[0]
    slots, points, cells = disk_filter.shape[2:]
    turbines = turbine_owner.shape[0]
    rows = comps * sx * sy
    lanes = -(-turbines // 128) * 128
    packed = comps * max(sx, sy) * levels // 128
    halves = levels // 128
    dims = (ngx, ngy, comps, sx, sy, steps, slots, points, turbines)
    anywhere = pl.BlockSpec(memory_space=pl.ANY)
    halo = pltpu.VMEM((steps, 4, packed, 128), BF16)
    dma = pltpu.SemaphoreType.DMA
    final, totals = pl.pallas_call(
        functools.partial(kernel, dims),
        out_shape=(
            jax.ShapeDtypeStruct((rows, levels), F32),
            jax.ShapeDtypeStruct((1, 1, turbines), F32),
        ),
        in_specs=[pl.BlockSpec(memory_space=pltpu.HBM)] * 7,
        out_specs=(anywhere, pl.BlockSpec(memory_space=pltpu.VMEM)),
        scratch_shapes=[
            pltpu.VMEM((halves, rows, 128), F32),
            pltpu.VMEM((saved, rows, levels), BF16),
            pltpu.SMEM(step_index.shape, jnp.int32),
            pltpu.VMEM((levels, levels), F32),
            pltpu.VMEM((slots * points, cells), BF16),
            pltpu.SMEM(pair_turbine.shape, jnp.int32),
            pltpu.SMEM(pair_tile.shape, jnp.int32),
            pltpu.VMEM((levels, levels), BF16),
            pltpu.VMEM((levels, levels), BF16),
            pltpu.VMEM((halves, rows, 128), F32),
            pltpu.VMEM((steps, halves, rows, 128), F32),
            pltpu.VMEM((sx * sy, levels), BF16),
            pltpu.VMEM((2 * slots, sx * sy), BF16),
            pltpu.VMEM((slots, slots * points), F32),
            pltpu.VMEM((slots, slots * points), F32),
            halo, halo, halo, halo,
            pltpu.VMEM((1, lanes), F32),
            pltpu.VMEM((ngy - 1, 1, lanes), F32),
            pltpu.VMEM((1, lanes), F32),
            pltpu.VMEM((ngx - 1, 1, lanes), F32),
            dma((6 + halves,)), dma((halves,)),
            dma((steps, 4)), dma((steps, 4)), dma((steps, 4)), dma((steps, 4)),
            dma((ngy - 1,)), dma((ngy - 1,)), dma((ngx - 1,)), dma((ngx - 1,)),
        ],
        compiler_params=pltpu.CompilerParams(
            collective_id=0, has_side_effects=True, vmem_limit_bytes=60 * 1024 * 1024
        ),
        name="sweep",
    )(
        adjoint_init.reshape(rows, levels),
        saved_states.reshape(saved, rows, levels),
        step_index,
        vertical_inverse,
        disk_filter.reshape(slots * points, cells),
        pair_turbine,
        pair_tile,
    )
    own = lax.axis_index("gx") * ngy + lax.axis_index("gy")
    grad = jnp.where(turbine_owner[None, None, :] == own, totals, 0.0)
    return final.reshape(adjoint_init.shape), grad


def solution(mesh):
    placed = (
        P(None, "gx", "gy", None),
        P(None, None, "gx", "gy", None),
        P(),
        P(),
        P("gx", "gy", None, None, None),
        P("gx", "gy", None),
        P("gx", "gy", None),
        P(),
    )
    return jax.shard_map(
        functools.partial(body, (mesh.shape["gx"], mesh.shape["gy"])),
        mesh=mesh,
        in_specs=placed,
        out_specs=(P(None, "gx", "gy", None), P("gx", "gy", None)),
        check_vma=False,
    )
```

```python
import functools

import jax
import jax.numpy as jnp
from jax import lax
from jax.experimental import pallas as pl
from jax.experimental.pallas import tpu as pltpu
from jax.sharding import PartitionSpec as P

COURANT = 0.2
HALF = 0.5 * COURANT
MESH = pl.DeviceIdType.MESH
F32 = jnp.float32
BF16 = jnp.bfloat16


def pack(rows):
    parts = [rows[:, k : k + 128] for k in range(0, rows.shape[1], 128)]
    return jnp.concatenate(parts, axis=0).astype(BF16)


def unpack(packed, count):
    wide = packed.astype(F32)
    return jnp.concatenate(
        [wide[k : k + count] for k in range(0, wide.shape[0], count)], axis=1
    )


def read(view, rows):
    return jnp.concatenate([view[k, rows, :] for k in range(view.shape[0])], axis=1)


def write(view, rows, value):
    for k in range(view.shape[0]):
        view[k, rows, :] = value[:, 128 * k : 128 * (k + 1)]


def row_diff(tile, low=0.0, high=0.0):
    size = tile.shape[0]
    place = lax.broadcasted_iota(jnp.int32, tile.shape, 0)
    above = jnp.where(place == size - 1, high, pltpu.roll(tile, size - 1, 0))
    below = jnp.where(place == 0, low, pltpu.roll(tile, 1, 0))
    return above - below


def split(wide):
    return [wide[:, k : k + 128] for k in range(0, wide.shape[1], 128)]


def depth_diff(tiles):
    place = lax.broadcasted_iota(jnp.int32, tiles[0].shape, 1)
    ups = [pltpu.roll(tile, 127, 1) for tile in tiles] + [0.0]
    downs = [0.0] + [pltpu.roll(tile, 1, 1) for tile in tiles]
    return [
        jnp.where(place == 127, ups[k + 1], ups[k]) - jnp.where(place == 0, downs[k], downs[k + 1])
        for k in range(len(tiles))
    ]


def kernel(
    dims,
    init_hbm, states_hbm, index_hbm, inverse_hbm, filter_hbm, turbine_hbm, tile_hbm,
    out_hbm, total_ref,
    adj, states, index_s, inverse, filters, turbine_s, tile_s,
    inv_hi, inv_lo, solved, vel, history, pick, weight, terms,
    send_v, recv_v, send_s, recv_s, send_c, recv_c,
    part, got,
    load_sem, out_sem, sv_sem, rv_sem, ss_sem, rs_sem, sc_sem, rc_sem, st_sem, rt_sem,
):
    ngx, ngy, comps, sx, sy, steps, slots, points, turbines = dims
    cols = sx * sy
    halves = adj.shape[0]
    levels = 128 * halves
    everything = pl.ds(0, comps * cols)
    gx, gy = lax.axis_index("gx"), lax.axis_index("gy")

    loads = [
        pltpu.make_async_copy(src, dst, load_sem.at[k])
        for k, (src, dst) in enumerate((
            (index_hbm, index_s), (states_hbm, states), (inverse_hbm, inverse),
            (turbine_hbm, turbine_s), (tile_hbm, tile_s), (filter_hbm, filters),
            *((init_hbm.at[:, pl.ds(128 * k, 128)], adj.at[k]) for k in range(halves)),
        ))
    ]
    for load in loads:
        load.start()

    barrier = pltpu.get_barrier_semaphore()

    count = ngx * ngy
    me = gx * ngy + gy

    def peer(k):
        other = lax.rem(me + k, count)
        return (other // ngy, lax.rem(other, ngy))

    def greet(k, c):
        pl.semaphore_signal(barrier, inc=1, device_id=peer(k), device_id_type=MESH)
        return c

    lax.fori_loop(1, count, greet, 0)

    beside_x = (lax.rem(gx + ngx - 1, ngx), lax.rem(gx + 1, ngx))
    beside_y = (lax.rem(gy + ngy - 1, ngy), lax.rem(gy + 1, ngy))
    beside = [(x, gy) for x in beside_x] + [(gx, y) for y in beside_y]
    aslant = [(x, y) for x in beside_x for y in beside_y]

    def edge(c, side, depth):
        base = c * cols
        if side == 0:
            return pl.ds(base + depth * sy, sy)
        if side == 1:
            return pl.ds(base + cols - (depth + 1) * sy, sy)
        return pl.ds(base + (depth if side == 2 else sy - 1 - depth), sx, stride=sy)

    def take(view, c, side, depth=0):
        return read(view, edge(c, side, depth))

    def put(view, c, side, value):
        write(view, edge(c, side, 0), value)

    def strips(view, side, depths):
        return [take(view, c, side, depth) for depth in depths for c in range(comps)]

    def stage_speed(r):
        for s in (2 * r, 2 * r + 1):
            write(vel.at[s], everything, states[index_s[s]].astype(F32))
        for side in range(4):
            parts = strips(vel.at[2 * r], side, (0, 1)) + strips(vel.at[2 * r + 1], side, (0,))
            send_v[r, side] = pack(jnp.concatenate(parts, axis=0))

    def stage_solved(r):
        for side in range(4):
            send_s[r, side] = pack(jnp.concatenate(strips(solved, side, (0, 1)), axis=0))
        place = lax.broadcasted_iota(jnp.int32, (8, 128), 0)
        for q in range(4):
            cell = (q // 2) * (sx - 1) * sy + (q % 2) * (sy - 1)
            tiles = []
            for k in range(halves):
                tile = jnp.zeros((8, 128), F32)
                for c in range(comps):
                    row = pl.ds(c * cols + cell, 1)
                    tile = jnp.where(place == c, solved[k, row, :], tile)
                    tile = jnp.where(place == comps + c, vel[2 * r, k, row, :], tile)
                tiles.append(tile)
            send_c[r, q] = jnp.concatenate(tiles, axis=0).astype(BF16)

    def remote(staging, landing, ssem, rsem, r, k, flip, where):
        return pltpu.make_async_remote_copy(
            src_ref=staging.at[r, k],
            dst_ref=landing.at[r, k ^ flip],
            send_sem=ssem.at[r, k],
            recv_sem=rsem.at[r, k ^ flip],
            device_id=where[k],
            device_id_type=MESH,
        )

    def speed_copy(r, side):
        return remote(send_v, recv_v, sv_sem, rv_sem, r, side, 1, beside)

    def solved_copy(r, side):
        return remote(send_s, recv_s, ss_sem, rs_sem, r, side, 1, beside)

    def corner_copy(r, q):
        return remote(send_c, recv_c, sc_sem, rc_sem, r, q, 3, aslant)

    def split_corner(packed):
        wide = packed.astype(F32)
        return [wide[8 * k : 8 * (k + 1)] for k in range(halves)]

    def product(value):
        hi = value.astype(BF16)
        lo = (value - hi.astype(F32)).astype(BF16)
        dot = functools.partial(jnp.dot, preferred_element_type=F32)
        return dot(hi, inv_hi[...]) + (dot(hi, inv_lo[...]) + dot(lo, inv_hi[...]))

    def local(s):
        def field(view, c, x):
            if x < 0 or x >= sx:
                return [jnp.zeros((sy, 128), F32)] * halves
            return [view[k, pl.ds(c * cols + x * sy, sy), :] for k in range(halves)]

        def diffs(view, c, x):
            mid = field(view, c, x)
            low, high = field(view, c, x - 1), field(view, c, x + 1)
            return (
                [high[k] - low[k] for k in range(halves)],
                [row_diff(tile) for tile in mid],
                depth_diff(mid),
            )

        speed = vel.at[s]
        for x in range(sx):
            speeds = [field(speed, c, x) for c in range(comps)]
            now = [field(solved, c, x) for c in range(comps)]
            slopes = [diffs(speed, c, x) for c in range(comps)]
            for c in range(comps):
                own = diffs(solved, c, x)
                for k in range(halves):
                    total = speeds[0][k] * own[0][k] - now[0][k] * slopes[0][c][k]
                    for d in range(1, comps):
                        total = total + speeds[d][k] * own[d][k]
                        total = total - now[d][k] * slopes[d][c][k]
                    adj[k, pl.ds(c * cols + x * sy, sy), :] = now[c][k] + HALF * total

    def triples(packed, side):
        width = sy if side < 2 else sx
        wide = unpack(packed, packed.shape[0] // halves)
        return [
            [split(wide[i + c * width : i + (c + 1) * width]) for c in range(comps)]
            for i in range(0, wide.shape[0], comps * width)
        ]

    def fix(s, side, far, far_speed):
        sign = -HALF if side % 2 == 0 else HALF
        across = side // 2
        rows = edge(0, side, 0)
        for k in range(halves):
            at = lambda view, c: view[k, edge(c, side, 0), :]
            carrier = sign * at(vel.at[s], across)
            for c in range(comps):
                new = at(adj, c) + carrier * far[c][k]
                if c == across:
                    total = at(solved, 0) * far_speed[0][k]
                    for d in range(1, comps):
                        total = total + at(solved, d) * far_speed[d][k]
                    new = new - sign * total
                adj[k, edge(c, side, 0), :] = new

    def outside(r, side, far, far_speed, corners):
        across, along = side // 2, 1 - side // 2
        ends = (2 * (side % 2), 2 * (side % 2) + 1) if across == 0 else (side % 2, 2 + side % 2)

        def normal(inner, outer):
            return [(i - o) if side % 2 == 0 else (o - i) for i, o in zip(inner, outer)]

        def diffs(c, view, strip, base):
            mid, outer = strip[0][c], strip[1][c]
            slopes = [None] * 3
            slopes[across] = normal(split(take(view, c, side)), outer)
            row = base + c
            slopes[along] = [
                row_diff(
                    mid[k],
                    corners[ends[0]][k][row : row + 1],
                    corners[ends[1]][k][row : row + 1],
                )
                for k in range(halves)
            ]
            slopes[2] = depth_diff(mid)
            return slopes

        own = [diffs(c, solved, far, 0) for c in range(comps)]
        speed = [diffs(c, vel.at[2 * r], far_speed, comps) for c in range(comps)]
        news = []
        for c in range(comps):
            tiles = []
            for k in range(halves):
                total = far_speed[0][0][k] * own[c][0][k] - far[0][0][k] * speed[0][c][k]
                for d in range(1, comps):
                    total = total + far_speed[0][d][k] * own[c][d][k]
                    total = total - far[0][d][k] * speed[d][c][k]
                tiles.append(far[0][c][k] + HALF * total)
            news.append(jnp.concatenate(tiles, axis=1))
        return news

    rows = lax.broadcasted_iota(jnp.int32, (2 * slots, cols), 0)
    places = lax.broadcasted_iota(jnp.int32, (2 * slots, cols), 1)
    lanes = got.shape[-1]
    span = slots * points
    slot_row = lax.broadcasted_iota(jnp.int32, (slots, span), 0) * points
    slot_col = lax.broadcasted_iota(jnp.int32, (slots, span), 1)
    inside = (slot_col >= slot_row) & (slot_col < slot_row + points)

    def look(sources):
        vectors = []
        for source in sources:
            found = jnp.dot(pick[...], source, preferred_element_type=F32)
            vectors.append(jnp.concatenate([found[:slots], found[slots:]], axis=1))
        stacked = vectors[0] if len(vectors) == 1 else jnp.concatenate(vectors, axis=0)
        return lax.dot_general(
            stacked.astype(BF16), filters[...], (((1,), (1,)), ((), ())), preferred_element_type=F32
        )

    loads[2].wait()
    whole = inverse[...]
    high = whole.astype(BF16)
    inv_hi[...] = high
    inv_lo[...] = (whole - high.astype(F32)).astype(BF16)
    for load in loads[6:]:
        load.wait()
    write(solved, everything, product(read(adj, everything)))
    loads[0].wait()
    loads[1].wait()
    stage_speed(0)
    stage_solved(0)

    pl.semaphore_wait(barrier, count - 1)
    for k in range(4):
        solved_copy(0, k).start()
        corner_copy(0, k).start()
        speed_copy(0, k).start()

    for load in loads[3:6]:
        load.wait()
    wanted = jnp.zeros((2 * slots, cols), jnp.int32)
    for j in range(slots):
        first = 2 * tile_s[0, 0, j]
        wanted = jnp.where(rows == j, first, wanted)
        wanted = jnp.where(rows == slots + j, first + 1, wanted)
    pick[...] = jnp.where(wanted == places, 1.0, 0.0).astype(BF16)
    history[...] = jnp.zeros_like(history)
    weight[...] = jnp.zeros_like(weight)
    terms[...] = jnp.zeros_like(terms)

    def pair(r, carry):
        first, second = 2 * r, 2 * r + 1

        @pl.when(r < steps // 2 - 1)
        def _():
            stage_speed(r + 1)
            for side in range(4):
                speed_copy(r + 1, side).start()

        local(first)
        sources = [history[i] for i in range(2)]
        sources += [read(vel.at[s], pl.ds(0, cols)).astype(BF16) for s in (first, second)]
        seen = look(sources)
        parts = [seen[i * slots : (i + 1) * slots] for i in range(4)]
        terms[...] += weight[0] * parts[0] + weight[1] * parts[1]
        for i in range(2):
            weight[i] = jnp.where(inside, parts[2 + i] * parts[2 + i], 0.0) * (1.0 / points)

        for k in range(4):
            speed_copy(r, k ^ 1).wait_recv()
            corner_copy(r, k ^ 3).wait_recv()
            solved_copy(r, k ^ 1).wait_recv()
        corners = [split_corner(recv_c[r, q]) for q in range(4)]
        ring = []
        for side in range(4):
            far = triples(recv_s[r, side], side)
            far_speed = triples(recv_v[r, side], side)
            fix(first, side, far[0], far_speed[0])
            ring += outside(r, side, far, far_speed, corners)
        history[0] = read(adj, pl.ds(0, cols)).astype(BF16)
        outer = product(jnp.concatenate(ring, axis=0))
        write(solved, everything, product(read(adj, everything)))

        local(second)
        start = 0
        for side in range(4):
            width = sy if side < 2 else sx
            far = [split(outer[start + c * width : start + (c + 1) * width]) for c in range(comps)]
            start += comps * width
            fix(second, side, far, triples(recv_v[r, side], side)[2])
        history[1] = read(adj, pl.ds(0, cols)).astype(BF16)

        @pl.when(r < steps // 2 - 1)
        def _():
            write(solved, everything, product(read(adj, everything)))
            stage_solved(r + 1)
            for k in range(4):
                solved_copy(r + 1, k).start()
                corner_copy(r + 1, k).start()

        return carry

    lax.fori_loop(0, steps // 2, pair, 0)

    outs = [
        pltpu.make_async_copy(adj.at[k], out_hbm.at[:, pl.ds(128 * k, 128)], out_sem.at[k])
        for k in range(halves)
    ]
    for out in outs:
        out.start()

    seen = look([history[i] for i in range(2)])
    total = terms[...] + weight[0] * seen[:slots] + weight[1] * seen[slots:]
    term = jnp.sum(total, axis=1, keepdims=True)
    slot_rows = lax.broadcasted_iota(jnp.int32, (slots, lanes), 0)
    lane = lax.broadcasted_iota(jnp.int32, (slots, lanes), 1)
    named = jnp.full((slots, lanes), turbines, jnp.int32)
    for j in range(slots):
        named = jnp.where(slot_rows == j, turbine_s[0, 0, j], named)
    live = (named == lane) & (lane < turbines)
    part[...] = jnp.sum(jnp.where(live, term, 0.0), axis=0, keepdims=True)

    def share(k):
        return pltpu.make_async_remote_copy(
            src_ref=part, dst_ref=got.at[k - 1],
            send_sem=st_sem.at[k - 1], recv_sem=rt_sem.at[k - 1],
            device_id=peer(k), device_id_type=MESH,
        )

    def run(act):
        def one(k, c):
            act(share(k))
            return c
        lax.fori_loop(1, count, one, 0)

    run(lambda c: c.start())

    def drain(r, c):
        for k in range(4):
            speed_copy(r, k).wait_send()
            solved_copy(r, k).wait_send()
            corner_copy(r, k).wait_send()
        return c

    lax.fori_loop(0, steps // 2, drain, 0)
    run(lambda c: c.wait_recv())
    summed = part[...] + jnp.sum(got[...], axis=0)
    total_ref[...] = summed[:, :turbines].reshape(total_ref.shape)
    run(lambda c: c.wait_send())
    for out in outs:
        out.wait()


def body(sizes, adjoint_init, saved_states, step_index, vertical_inverse, disk_filter,
         pair_turbine, pair_tile, turbine_owner):
    ngx, ngy = sizes
    comps, sx, sy, levels = adjoint_init.shape
    saved = saved_states.shape[0]
    steps = step_index.shape[0]
    slots, points, cells = disk_filter.shape[2:]
    turbines = turbine_owner.shape[0]
    rows = comps * sx * sy
    lanes = -(-turbines // 128) * 128
    strip = comps * max(sx, sy) * levels // 128
    halves = levels // 128
    rounds = steps // 2
    count = ngx * ngy
    assert steps % 2 == 0 and sx == sy
    dims = (ngx, ngy, comps, sx, sy, steps, slots, points, turbines)
    anywhere = pl.BlockSpec(memory_space=pl.ANY)
    halo = lambda rows: pltpu.VMEM((rounds, 4, rows, 128), BF16)
    dma = pltpu.SemaphoreType.DMA
    final, totals = pl.pallas_call(
        functools.partial(kernel, dims),
        out_shape=(
            jax.ShapeDtypeStruct((rows, levels), F32),
            jax.ShapeDtypeStruct((1, 1, turbines), F32),
        ),
        in_specs=[pl.BlockSpec(memory_space=pltpu.HBM)] * 7,
        out_specs=(anywhere, pl.BlockSpec(memory_space=pltpu.VMEM)),
        scratch_shapes=[
            pltpu.VMEM((halves, rows, 128), F32),
            pltpu.VMEM((saved, rows, levels), BF16),
            pltpu.SMEM(step_index.shape, jnp.int32),
            pltpu.VMEM((levels, levels), F32),
            pltpu.VMEM((slots * points, cells), BF16),
            pltpu.SMEM(pair_turbine.shape, jnp.int32),
            pltpu.SMEM(pair_tile.shape, jnp.int32),
            pltpu.VMEM((levels, levels), BF16),
            pltpu.VMEM((levels, levels), BF16),
            pltpu.VMEM((halves, rows, 128), F32),
            pltpu.VMEM((steps, halves, rows, 128), F32),
            pltpu.VMEM((2, sx * sy, levels), BF16),
            pltpu.VMEM((2 * slots, sx * sy), BF16),
            pltpu.VMEM((2, slots, slots * points), F32),
            pltpu.VMEM((slots, slots * points), F32),
            halo(3 * strip), halo(3 * strip), halo(2 * strip), halo(2 * strip),
            halo(8 * halves), halo(8 * halves),
            pltpu.VMEM((1, lanes), F32),
            pltpu.VMEM((count - 1, 1, lanes), F32),
            dma((6 + halves,)), dma((halves,)),
            *[dma((rounds, 4))] * 6,
            dma((count - 1,)), dma((count - 1,)),
        ],
        compiler_params=pltpu.CompilerParams(
            collective_id=0, has_side_effects=True, vmem_limit_bytes=60 * 1024 * 1024
        ),
        name="sweep",
    )(
        adjoint_init.reshape(rows, levels),
        saved_states.reshape(saved, rows, levels),
        step_index,
        vertical_inverse,
        disk_filter.reshape(slots * points, cells),
        pair_turbine,
        pair_tile,
    )
    own = lax.axis_index("gx") * ngy + lax.axis_index("gy")
    grad = jnp.where(turbine_owner[None, None, :] == own, totals, 0.0)
    return final.reshape(adjoint_init.shape), grad


def solution(mesh):
    placed = (
        P(None, "gx", "gy", None),
        P(None, None, "gx", "gy", None),
        P(),
        P(),
        P("gx", "gy", None, None, None),
        P("gx", "gy", None),
        P("gx", "gy", None),
        P(),
    )
    return jax.shard_map(
        functools.partial(body, (mesh.shape["gx"], mesh.shape["gy"])),
        mesh=mesh,
        in_specs=placed,
        out_specs=(P(None, "gx", "gy", None), P("gx", "gy", None)),
        check_vma=False,
    )
```

```python
import functools

import jax
import jax.numpy as jnp
from jax import lax
from jax.experimental import pallas as pl
from jax.experimental.pallas import tpu as pltpu
from jax.sharding import PartitionSpec as P

COURANT = 0.2
HALF = 0.5 * COURANT
MESH = pl.DeviceIdType.MESH
F32 = jnp.float32
BF16 = jnp.bfloat16


def pack(rows):
    parts = [rows[:, k : k + 128] for k in range(0, rows.shape[1], 128)]
    return jnp.concatenate(parts, axis=0).astype(BF16)


def unpack(packed, count):
    wide = packed.astype(F32)
    return jnp.concatenate(
        [wide[k : k + count] for k in range(0, wide.shape[0], count)], axis=1
    )


def read(view, rows):
    return jnp.concatenate([view[k, rows, :] for k in range(view.shape[0])], axis=1)


def write(view, rows, value):
    for k in range(view.shape[0]):
        view[k, rows, :] = value[:, 128 * k : 128 * (k + 1)]


def row_diff(tile, low=0.0, high=0.0):
    size = tile.shape[0]
    place = lax.broadcasted_iota(jnp.int32, tile.shape, 0)
    above = jnp.where(place == size - 1, high, pltpu.roll(tile, size - 1, 0))
    below = jnp.where(place == 0, low, pltpu.roll(tile, 1, 0))
    return above - below


def split(wide):
    return [wide[:, k : k + 128] for k in range(0, wide.shape[1], 128)]


def depth_diff(tiles):
    place = lax.broadcasted_iota(jnp.int32, tiles[0].shape, 1)
    ups = [pltpu.roll(tile, 127, 1) for tile in tiles] + [0.0]
    downs = [0.0] + [pltpu.roll(tile, 1, 1) for tile in tiles]
    return [
        jnp.where(place == 127, ups[k + 1], ups[k]) - jnp.where(place == 0, downs[k], downs[k + 1])
        for k in range(len(tiles))
    ]


def kernel(
    dims,
    init_hbm, states_hbm, index_hbm, inverse_hbm, filter_hbm, turbine_hbm, tile_hbm, owner_hbm,
    out_hbm, grad_hbm,
    adj, states, index_s, inverse, filters, turbine_s, tile_s, owner_s,
    inv_hi, inv_lo, solved, vel, history, pick, live, mine, weight, terms, grad,
    send_v, recv_v, send_w, recv_w, send_s, recv_s, send_c, recv_c,
    part, got,
    load_sem, out_sem, sv_sem, rv_sem, sw_sem, rw_sem, ss_sem, rs_sem, sc_sem, rc_sem, st_sem, rt_sem,
):
    ngx, ngy, comps, sx, sy, steps, slots, points, turbines = dims
    cols = sx * sy
    halves = adj.shape[0]
    levels = 128 * halves
    everything = pl.ds(0, comps * cols)
    gx, gy = lax.axis_index("gx"), lax.axis_index("gy")

    loads = [
        pltpu.make_async_copy(src, dst, load_sem.at[k])
        for k, (src, dst) in enumerate((
            *((init_hbm.at[:, pl.ds(128 * k, 128)], adj.at[k]) for k in range(halves)),
            (inverse_hbm, inverse), (index_hbm, index_s), (states_hbm, states),
            (turbine_hbm, turbine_s), (tile_hbm, tile_s), (owner_hbm, owner_s), (filter_hbm, filters),
        ))
    ]
    for load in loads:
        load.start()

    barrier = pltpu.get_barrier_semaphore()

    count = ngx * ngy
    me = gx * ngy + gy

    def peer(k):
        if isinstance(k, int):
            x, y = gx + k // ngy, gy + k % ngy
            return (jnp.where(x >= ngx, x - ngx, x), jnp.where(y >= ngy, y - ngy, y))
        return (lax.rem(gx + k // ngy, ngx), lax.rem(gy + lax.rem(k, ngy), ngy))

    def others(act):
        if count <= 64:
            for k in range(1, count):
                act(k)
        else:
            def one(k, c):
                act(k)
                return c
            lax.fori_loop(1, count, one, 0)

    others(lambda k: pl.semaphore_signal(barrier, inc=1, device_id=peer(k), device_id_type=MESH))

    beside_x = (lax.rem(gx + ngx - 1, ngx), lax.rem(gx + 1, ngx))
    beside_y = (lax.rem(gy + ngy - 1, ngy), lax.rem(gy + 1, ngy))
    beside = [(x, gy) for x in beside_x] + [(gx, y) for y in beside_y]
    aslant = [(x, y) for x in beside_x for y in beside_y]

    def edge(c, side, depth):
        base = c * cols
        if side == 0:
            return pl.ds(base + depth * sy, sy)
        if side == 1:
            return pl.ds(base + cols - (depth + 1) * sy, sy)
        return pl.ds(base + (depth if side == 2 else sy - 1 - depth), sx, stride=sy)

    def take(view, c, side, depth=0):
        return read(view, edge(c, side, depth))

    def put(view, c, side, value):
        write(view, edge(c, side, 0), value)

    def strips(view, side, depths):
        return [take(view, c, side, depth) for depth in depths for c in range(comps)]

    def stage_speed(r):
        for s in (2 * r, 2 * r + 1):
            write(vel.at[s], everything, states[index_s[s]].astype(F32))
        for side in range(4):
            send_v[r, side] = pack(jnp.concatenate(strips(vel.at[2 * r], side, (0, 1)), axis=0))
            send_w[r, side] = pack(jnp.concatenate(strips(vel.at[2 * r + 1], side, (0,)), axis=0))

    def stage_solved(r):
        for side in range(4):
            send_s[r, side] = pack(jnp.concatenate(strips(solved, side, (0, 1)), axis=0))
        place = lax.broadcasted_iota(jnp.int32, (8, 128), 0)
        for q in range(4):
            cell = (q // 2) * (sx - 1) * sy + (q % 2) * (sy - 1)
            tiles = []
            for k in range(halves):
                tile = jnp.zeros((8, 128), F32)
                for c in range(comps):
                    row = pl.ds(c * cols + cell, 1)
                    tile = jnp.where(place == c, solved[k, row, :], tile)
                    tile = jnp.where(place == comps + c, vel[2 * r, k, row, :], tile)
                tiles.append(tile)
            send_c[r, q] = jnp.concatenate(tiles, axis=0).astype(BF16)

    def remote(staging, landing, ssem, rsem, r, k, flip, where):
        return pltpu.make_async_remote_copy(
            src_ref=staging.at[r, k],
            dst_ref=landing.at[r, k ^ flip],
            send_sem=ssem.at[r, k],
            recv_sem=rsem.at[r, k ^ flip],
            device_id=where[k],
            device_id_type=MESH,
        )

    def speed_copy(r, side):
        return remote(send_v, recv_v, sv_sem, rv_sem, r, side, 1, beside)

    def later_copy(r, side):
        return remote(send_w, recv_w, sw_sem, rw_sem, r, side, 1, beside)

    def solved_copy(r, side):
        return remote(send_s, recv_s, ss_sem, rs_sem, r, side, 1, beside)

    def corner_copy(r, q):
        return remote(send_c, recv_c, sc_sem, rc_sem, r, q, 3, aslant)

    def split_corner(packed):
        wide = packed.astype(F32)
        return [wide[8 * k : 8 * (k + 1)] for k in range(halves)]

    def product(value):
        hi = value.astype(BF16)
        lo = (value - hi.astype(F32)).astype(BF16)
        dot = functools.partial(jnp.dot, preferred_element_type=F32)
        return dot(hi, inv_hi[...]) + (dot(hi, inv_lo[...]) + dot(lo, inv_hi[...]))

    def local(s):
        def field(view, c, x):
            if x < 0 or x >= sx:
                return [jnp.zeros((sy, 128), F32)] * halves
            return [view[k, pl.ds(c * cols + x * sy, sy), :] for k in range(halves)]

        def diffs(view, c, x):
            mid = field(view, c, x)
            low, high = field(view, c, x - 1), field(view, c, x + 1)
            return (
                [high[k] - low[k] for k in range(halves)],
                [row_diff(tile) for tile in mid],
                depth_diff(mid),
            )

        speed = vel.at[s]
        for x in range(sx):
            speeds = [field(speed, c, x) for c in range(comps)]
            now = [field(solved, c, x) for c in range(comps)]
            slopes = [diffs(speed, c, x) for c in range(comps)]
            for c in range(comps):
                own = diffs(solved, c, x)
                for k in range(halves):
                    total = speeds[0][k] * own[0][k] - now[0][k] * slopes[0][c][k]
                    for d in range(1, comps):
                        total = total + speeds[d][k] * own[d][k]
                        total = total - now[d][k] * slopes[d][c][k]
                    adj[k, pl.ds(c * cols + x * sy, sy), :] = now[c][k] + HALF * total

    def triples(packed, side):
        width = sy if side < 2 else sx
        wide = unpack(packed, packed.shape[0] // halves)
        return [
            [split(wide[i + c * width : i + (c + 1) * width]) for c in range(comps)]
            for i in range(0, wide.shape[0], comps * width)
        ]

    def fix(s, side, far, far_speed):
        sign = -HALF if side % 2 == 0 else HALF
        across = side // 2
        rows = edge(0, side, 0)
        for k in range(halves):
            at = lambda view, c: view[k, edge(c, side, 0), :]
            carrier = sign * at(vel.at[s], across)
            for c in range(comps):
                new = at(adj, c) + carrier * far[c][k]
                if c == across:
                    total = at(solved, 0) * far_speed[0][k]
                    for d in range(1, comps):
                        total = total + at(solved, d) * far_speed[d][k]
                    new = new - sign * total
                adj[k, edge(c, side, 0), :] = new

    def outside(r, side, far, far_speed, corners):
        across, along = side // 2, 1 - side // 2
        ends = (2 * (side % 2), 2 * (side % 2) + 1) if across == 0 else (side % 2, 2 + side % 2)

        def normal(inner, outer):
            return [(i - o) if side % 2 == 0 else (o - i) for i, o in zip(inner, outer)]

        def diffs(c, view, strip, base):
            mid, outer = strip[0][c], strip[1][c]
            slopes = [None] * 3
            slopes[across] = normal(split(take(view, c, side)), outer)
            row = base + c
            slopes[along] = [
                row_diff(
                    mid[k],
                    corners[ends[0]][k][row : row + 1],
                    corners[ends[1]][k][row : row + 1],
                )
                for k in range(halves)
            ]
            slopes[2] = depth_diff(mid)
            return slopes

        own = [diffs(c, solved, far, 0) for c in range(comps)]
        speed = [diffs(c, vel.at[2 * r], far_speed, comps) for c in range(comps)]
        news = []
        for c in range(comps):
            tiles = []
            for k in range(halves):
                total = far_speed[0][0][k] * own[c][0][k] - far[0][0][k] * speed[0][c][k]
                for d in range(1, comps):
                    total = total + far_speed[0][d][k] * own[c][d][k]
                    total = total - far[0][d][k] * speed[d][c][k]
                tiles.append(far[0][c][k] + HALF * total)
            news.append(jnp.concatenate(tiles, axis=1))
        return news

    rows = lax.broadcasted_iota(jnp.int32, (2 * slots, cols), 0)
    places = lax.broadcasted_iota(jnp.int32, (2 * slots, cols), 1)
    lanes = got.shape[-1]
    span = slots * points
    slot_row = lax.broadcasted_iota(jnp.int32, (slots, span), 0) * points
    slot_col = lax.broadcasted_iota(jnp.int32, (slots, span), 1)
    inside = (slot_col >= slot_row) & (slot_col < slot_row + points)

    def look(sources):
        vectors = []
        for source in sources:
            found = jnp.dot(pick[...], source, preferred_element_type=F32)
            vectors.append(jnp.concatenate([found[:slots], found[slots:]], axis=1))
        stacked = vectors[0] if len(vectors) == 1 else jnp.concatenate(vectors, axis=0)
        return lax.dot_general(
            stacked.astype(BF16), filters[...], (((1,), (1,)), ((), ())), preferred_element_type=F32
        )

    loads[halves].wait()
    whole = inverse[...]
    high = whole.astype(BF16)
    inv_hi[...] = high
    inv_lo[...] = (whole - high.astype(F32)).astype(BF16)
    for load in loads[:halves]:
        load.wait()
    write(solved, everything, product(read(adj, everything)))
    loads[halves + 1].wait()
    loads[halves + 2].wait()
    stage_speed(0)
    stage_solved(0)

    pl.semaphore_wait(barrier, count - 1)
    for k in range(4):
        solved_copy(0, k).start()
        corner_copy(0, k).start()
        speed_copy(0, k).start()
    for k in range(4):
        later_copy(0, k).start()

    for load in loads[halves + 3 :]:
        load.wait()
    wanted = jnp.zeros((2 * slots, cols), jnp.int32)
    for j in range(slots):
        first = 2 * tile_s[0, 0, j]
        wanted = jnp.where(rows == j, first, wanted)
        wanted = jnp.where(rows == slots + j, first + 1, wanted)
    pick[...] = jnp.where(wanted == places, 1.0, 0.0).astype(BF16)
    slot_rows = lax.broadcasted_iota(jnp.int32, (slots, lanes), 0)
    lane = lax.broadcasted_iota(jnp.int32, (slots, lanes), 1)
    named = jnp.full((slots, lanes), turbines, jnp.int32)
    for j in range(slots):
        named = jnp.where(slot_rows == j, turbine_s[0, 0, j], named)
    live[...] = jnp.where((named == lane) & (lane < turbines), 1.0, 0.0)
    lane_row = lax.broadcasted_iota(jnp.int32, (1, lanes), 1)
    owners = jnp.full((1, lanes), -1, jnp.int32)
    for k in range(turbines):
        owners = jnp.where(lane_row == k, owner_s[k], owners)
    mine[...] = jnp.where(owners == me, 1.0, 0.0)
    history[...] = jnp.zeros_like(history)
    weight[...] = jnp.zeros_like(weight)
    terms[...] = jnp.zeros_like(terms)

    def pair(r, carry):
        first, second = 2 * r, 2 * r + 1

        @pl.when(r < steps // 2 - 1)
        def _():
            stage_speed(r + 1)
            for side in range(4):
                speed_copy(r + 1, side).start()
            for side in range(4):
                later_copy(r + 1, side).start()

        local(first)
        sources = [history[i] for i in range(2)]
        sources += [read(vel.at[s], pl.ds(0, cols)).astype(BF16) for s in (first, second)]
        seen = look(sources)
        parts = [seen[i * slots : (i + 1) * slots] for i in range(4)]
        terms[...] += weight[0] * parts[0] + weight[1] * parts[1]
        for i in range(2):
            weight[i] = jnp.where(inside, parts[2 + i] * parts[2 + i], 0.0) * (1.0 / points)

        for k in range(4):
            speed_copy(r, k ^ 1).wait_recv()
            corner_copy(r, k ^ 3).wait_recv()
            solved_copy(r, k ^ 1).wait_recv()
        corners = [split_corner(recv_c[r, q]) for q in range(4)]
        ring = []
        for side in range(4):
            far = triples(recv_s[r, side], side)
            far_speed = triples(recv_v[r, side], side)
            fix(first, side, far[0], far_speed[0])
            ring += outside(r, side, far, far_speed, corners)
        history[0] = read(adj, pl.ds(0, cols)).astype(BF16)
        outer = product(jnp.concatenate(ring, axis=0))
        write(solved, everything, product(read(adj, everything)))

        local(second)
        start = 0
        for side in range(4):
            later_copy(r, side ^ 1).wait_recv()
            width = sy if side < 2 else sx
            far = [split(outer[start + c * width : start + (c + 1) * width]) for c in range(comps)]
            start += comps * width
            fix(second, side, far, triples(recv_w[r, side], side)[0])
        history[1] = read(adj, pl.ds(0, cols)).astype(BF16)

        @pl.when(r < steps // 2 - 1)
        def _():
            write(solved, everything, product(read(adj, everything)))
            stage_solved(r + 1)
            for k in range(4):
                solved_copy(r + 1, k).start()
                corner_copy(r + 1, k).start()

        return carry

    lax.fori_loop(0, steps // 2, pair, 0)

    outs = [
        pltpu.make_async_copy(adj.at[k], out_hbm.at[:, pl.ds(128 * k, 128)], out_sem.at[k])
        for k in range(halves)
    ]
    for out in outs:
        out.start()

    seen = look([history[i] for i in range(2)])
    total = terms[...] + weight[0] * seen[:slots] + weight[1] * seen[slots:]
    term = jnp.sum(total, axis=1, keepdims=True)
    part[...] = jnp.sum(live[...] * term, axis=0, keepdims=True)

    def share(k):
        return pltpu.make_async_remote_copy(
            src_ref=part, dst_ref=got.at[k - 1], send_sem=st_sem, recv_sem=rt_sem,
            device_id=peer(k), device_id_type=MESH,
        )

    others(lambda k: share(k).start())

    def drain(r, c):
        for k in range(4):
            speed_copy(r, k).wait_send()
            later_copy(r, k).wait_send()
            solved_copy(r, k).wait_send()
            corner_copy(r, k).wait_send()
        return c

    lax.fori_loop(0, steps // 2, drain, 0)
    pltpu.make_async_copy(got, got, st_sem).wait()
    pltpu.make_async_copy(got, got, rt_sem).wait()
    summed = part[...] + jnp.sum(got[...], axis=0)
    grad[...] = jnp.where(mine[...] > 0.0, summed, 0.0)[:, :turbines].reshape(grad.shape)
    last = pltpu.make_async_copy(grad, grad_hbm, out_sem.at[halves])
    last.start()
    last.wait()
    for out in outs:
        out.wait()


def hand_over(parts, chunk, final_in, grad_in, final_out, grad_out, sem):
    moves = [pltpu.make_async_copy(grad_in, grad_out, sem.at[parts])]
    for k in range(parts):
        rows = pl.ds(k * chunk, chunk)
        moves.append(pltpu.make_async_copy(final_in.at[rows], final_out.at[rows], sem.at[k]))
    for move in moves:
        move.start()
    for move in moves:
        move.wait()


def body(sizes, adjoint_init, saved_states, step_index, vertical_inverse, disk_filter,
         pair_turbine, pair_tile, turbine_owner):
    ngx, ngy = sizes
    comps, sx, sy, levels = adjoint_init.shape
    saved = saved_states.shape[0]
    steps = step_index.shape[0]
    slots, points, cells = disk_filter.shape[2:]
    turbines = turbine_owner.shape[0]
    rows = comps * sx * sy
    lanes = -(-turbines // 128) * 128
    strip = comps * max(sx, sy) * levels // 128
    halves = levels // 128
    rounds = steps // 2
    count = ngx * ngy
    assert steps % 2 == 0 and sx == sy
    dims = (ngx, ngy, comps, sx, sy, steps, slots, points, turbines)
    anywhere = pl.BlockSpec(memory_space=pl.ANY)
    halo = lambda rows: pltpu.VMEM((rounds, 4, rows, 128), BF16)
    dma = pltpu.SemaphoreType.DMA
    final, grad = pl.pallas_call(
        functools.partial(kernel, dims),
        out_shape=(
            jax.ShapeDtypeStruct((rows, levels), F32),
            jax.ShapeDtypeStruct((1, 1, turbines), F32),
        ),
        in_specs=[pl.BlockSpec(memory_space=pltpu.HBM)] * 8,
        out_specs=(anywhere, anywhere),
        scratch_shapes=[
            pltpu.VMEM((halves, rows, 128), F32),
            pltpu.VMEM((saved, rows, levels), BF16),
            pltpu.SMEM(step_index.shape, jnp.int32),
            pltpu.VMEM((levels, levels), F32),
            pltpu.VMEM((slots * points, cells), BF16),
            pltpu.SMEM(pair_turbine.shape, jnp.int32),
            pltpu.SMEM(pair_tile.shape, jnp.int32),
            pltpu.SMEM(turbine_owner.shape, jnp.int32),
            pltpu.VMEM((levels, levels), BF16),
            pltpu.VMEM((levels, levels), BF16),
            pltpu.VMEM((halves, rows, 128), F32),
            pltpu.VMEM((steps, halves, rows, 128), F32),
            pltpu.VMEM((2, sx * sy, levels), BF16),
            pltpu.VMEM((2 * slots, sx * sy), BF16),
            pltpu.VMEM((slots, lanes), F32),
            pltpu.VMEM((1, lanes), F32),
            pltpu.VMEM((2, slots, slots * points), F32),
            pltpu.VMEM((slots, slots * points), F32),
            pltpu.VMEM((1, 1, turbines), F32),
            halo(2 * strip), halo(2 * strip), halo(strip), halo(strip), halo(2 * strip), halo(2 * strip),
            halo(8 * halves), halo(8 * halves),
            pltpu.VMEM((1, lanes), F32),
            pltpu.VMEM((count - 1, 1, lanes), F32),
            dma((7 + halves,)), dma((halves + 1,)),
            *[dma((rounds, 4))] * 8,
            dma, dma,
        ],
        compiler_params=pltpu.CompilerParams(
            collective_id=0, has_side_effects=True, vmem_limit_bytes=60 * 1024 * 1024
        ),
        name="sweep",
    )(
        adjoint_init.reshape(rows, levels),
        saved_states.reshape(saved, rows, levels),
        step_index,
        vertical_inverse,
        disk_filter.reshape(slots * points, cells),
        pair_turbine,
        pair_tile,
        turbine_owner,
    )
    chunk = rows // comps
    final, grad = pl.pallas_call(
        functools.partial(hand_over, comps, chunk),
        out_shape=(
            jax.ShapeDtypeStruct((rows, levels), F32),
            jax.ShapeDtypeStruct((1, 1, turbines), F32),
        ),
        in_specs=[anywhere] * 2,
        out_specs=(anywhere, anywhere),
        scratch_shapes=[dma((comps + 1,))],
        compiler_params=pltpu.CompilerParams(vmem_limit_bytes=60 * 1024 * 1024),
        name="hand_over",
    )(final, grad)
    return final.reshape(adjoint_init.shape), grad


def solution(mesh):
    placed = (
        P(None, "gx", "gy", None),
        P(None, None, "gx", "gy", None),
        P(),
        P(),
        P("gx", "gy", None, None, None),
        P("gx", "gy", None),
        P("gx", "gy", None),
        P(),
    )
    return jax.shard_map(
        functools.partial(body, (mesh.shape["gx"], mesh.shape["gy"])),
        mesh=mesh,
        in_specs=placed,
        out_specs=(P(None, "gx", "gy", None), P("gx", "gy", None)),
        check_vma=False,
    )
```

```python
import functools

import jax
import jax.numpy as jnp
from jax import lax
from jax.experimental import pallas as pl
from jax.experimental.pallas import tpu as pltpu
from jax.sharding import PartitionSpec as P

COURANT = 0.2
HALF = 0.5 * COURANT
MESH = pl.DeviceIdType.MESH
F32 = jnp.float32
BF16 = jnp.bfloat16


def pack(rows):
    parts = [rows[:, k : k + 128] for k in range(0, rows.shape[1], 128)]
    return jnp.concatenate(parts, axis=0).astype(BF16)


def unpack(packed, count):
    wide = packed.astype(F32)
    return jnp.concatenate(
        [wide[k : k + count] for k in range(0, wide.shape[0], count)], axis=1
    )


def read(view, rows):
    return jnp.concatenate([view[k, rows, :] for k in range(view.shape[0])], axis=1)


def write(view, rows, value):
    for k in range(view.shape[0]):
        view[k, rows, :] = value[:, 128 * k : 128 * (k + 1)]


def row_diff(tile, low=0.0, high=0.0):
    size = tile.shape[0]
    place = lax.broadcasted_iota(jnp.int32, tile.shape, 0)
    above = jnp.where(place == size - 1, high, pltpu.roll(tile, size - 1, 0))
    below = jnp.where(place == 0, low, pltpu.roll(tile, 1, 0))
    return above - below


def split(wide):
    return [wide[:, k : k + 128] for k in range(0, wide.shape[1], 128)]


def depth_diff(tiles):
    place = lax.broadcasted_iota(jnp.int32, tiles[0].shape, 1)
    ups = [pltpu.roll(tile, 127, 1) for tile in tiles] + [0.0]
    downs = [0.0] + [pltpu.roll(tile, 1, 1) for tile in tiles]
    return [
        jnp.where(place == 127, ups[k + 1], ups[k]) - jnp.where(place == 0, downs[k], downs[k + 1])
        for k in range(len(tiles))
    ]


def kernel(
    dims,
    init_hbm, states_hbm, index_hbm, inverse_hbm, filter_hbm, turbine_hbm, tile_hbm, owner_hbm,
    out_ref, grad_ref,
    adj, states, index_s, inverse, filters, turbine_s, tile_s, owner_s,
    inv_hi, inv_lo, solved, vel, history, pick, live, mine, weight, terms,
    send_v, recv_v, send_w, recv_w, send_s, recv_s, send_c, recv_c,
    part, got,
    load_sem, sv_sem, rv_sem, sw_sem, rw_sem, ss_sem, rs_sem, sc_sem, rc_sem, st_sem, rt_sem,
):
    ngx, ngy, comps, sx, sy, steps, slots, points, turbines = dims
    cols = sx * sy
    halves = adj.shape[0]
    levels = 128 * halves
    everything = pl.ds(0, comps * cols)
    gx, gy = lax.axis_index("gx"), lax.axis_index("gy")

    loads = [
        pltpu.make_async_copy(src, dst, load_sem.at[k])
        for k, (src, dst) in enumerate((
            *((init_hbm.at[:, pl.ds(128 * k, 128)], adj.at[k]) for k in range(halves)),
            (inverse_hbm, inverse), (index_hbm, index_s), (states_hbm, states),
            (turbine_hbm, turbine_s), (tile_hbm, tile_s), (owner_hbm, owner_s), (filter_hbm, filters),
        ))
    ]
    for load in loads:
        load.start()

    barrier = pltpu.get_barrier_semaphore()

    count = ngx * ngy
    me = gx * ngy + gy

    def peer(k):
        if isinstance(k, int):
            x, y = gx + k // ngy, gy + k % ngy
            return (jnp.where(x >= ngx, x - ngx, x), jnp.where(y >= ngy, y - ngy, y))
        return (lax.rem(gx + k // ngy, ngx), lax.rem(gy + lax.rem(k, ngy), ngy))

    def others(act):
        if count <= 64:
            for k in range(1, count):
                act(k)
        else:
            def one(k, c):
                act(k)
                return c
            lax.fori_loop(1, count, one, 0)

    others(lambda k: pl.semaphore_signal(barrier, inc=1, device_id=peer(k), device_id_type=MESH))

    beside_x = (lax.rem(gx + ngx - 1, ngx), lax.rem(gx + 1, ngx))
    beside_y = (lax.rem(gy + ngy - 1, ngy), lax.rem(gy + 1, ngy))
    beside = [(x, gy) for x in beside_x] + [(gx, y) for y in beside_y]
    aslant = [(x, y) for x in beside_x for y in beside_y]

    def edge(c, side, depth):
        base = c * cols
        if side == 0:
            return pl.ds(base + depth * sy, sy)
        if side == 1:
            return pl.ds(base + cols - (depth + 1) * sy, sy)
        return pl.ds(base + (depth if side == 2 else sy - 1 - depth), sx, stride=sy)

    def take(view, c, side, depth=0):
        return read(view, edge(c, side, depth))

    def put(view, c, side, value):
        write(view, edge(c, side, 0), value)

    def strips(view, side, depths):
        return [take(view, c, side, depth) for depth in depths for c in range(comps)]

    def stage_speed(r):
        for s in (2 * r, 2 * r + 1):
            write(vel.at[s], everything, states[index_s[s]].astype(F32))
        for side in range(4):
            send_v[r, side] = pack(jnp.concatenate(strips(vel.at[2 * r], side, (0, 1)), axis=0))
            send_w[r, side] = pack(jnp.concatenate(strips(vel.at[2 * r + 1], side, (0,)), axis=0))

    def stage_solved(r):
        for side in range(4):
            send_s[r, side] = pack(jnp.concatenate(strips(solved, side, (0, 1)), axis=0))
        place = lax.broadcasted_iota(jnp.int32, (8, 128), 0)
        for q in range(4):
            cell = (q // 2) * (sx - 1) * sy + (q % 2) * (sy - 1)
            tiles = []
            for k in range(halves):
                tile = jnp.zeros((8, 128), F32)
                for c in range(comps):
                    row = pl.ds(c * cols + cell, 1)
                    tile = jnp.where(place == c, solved[k, row, :], tile)
                    tile = jnp.where(place == comps + c, vel[2 * r, k, row, :], tile)
                tiles.append(tile)
            send_c[r, q] = jnp.concatenate(tiles, axis=0).astype(BF16)

    def remote(staging, landing, ssem, rsem, r, k, flip, where):
        return pltpu.make_async_remote_copy(
            src_ref=staging.at[r, k],
            dst_ref=landing.at[r, k ^ flip],
            send_sem=ssem.at[r, k],
            recv_sem=rsem.at[r, k ^ flip],
            device_id=where[k],
            device_id_type=MESH,
        )

    def speed_copy(r, side):
        return remote(send_v, recv_v, sv_sem, rv_sem, r, side, 1, beside)

    def later_copy(r, side):
        return remote(send_w, recv_w, sw_sem, rw_sem, r, side, 1, beside)

    def solved_copy(r, side):
        return remote(send_s, recv_s, ss_sem, rs_sem, r, side, 1, beside)

    def corner_copy(r, q):
        return remote(send_c, recv_c, sc_sem, rc_sem, r, q, 3, aslant)

    def split_corner(packed):
        wide = packed.astype(F32)
        return [wide[8 * k : 8 * (k + 1)] for k in range(halves)]

    def product(value):
        hi = value.astype(BF16)
        lo = (value - hi.astype(F32)).astype(BF16)
        dot = functools.partial(jnp.dot, preferred_element_type=F32)
        return dot(hi, inv_hi[...]) + (dot(hi, inv_lo[...]) + dot(lo, inv_hi[...]))

    def local(s):
        def field(view, c, x):
            if x < 0 or x >= sx:
                return [jnp.zeros((sy, 128), F32)] * halves
            return [view[k, pl.ds(c * cols + x * sy, sy), :] for k in range(halves)]

        def diffs(view, c, x):
            mid = field(view, c, x)
            low, high = field(view, c, x - 1), field(view, c, x + 1)
            return (
                [high[k] - low[k] for k in range(halves)],
                [row_diff(tile) for tile in mid],
                depth_diff(mid),
            )

        speed = vel.at[s]
        for x in range(sx):
            speeds = [field(speed, c, x) for c in range(comps)]
            now = [field(solved, c, x) for c in range(comps)]
            slopes = [diffs(speed, c, x) for c in range(comps)]
            for c in range(comps):
                own = diffs(solved, c, x)
                for k in range(halves):
                    total = speeds[0][k] * own[0][k] - now[0][k] * slopes[0][c][k]
                    for d in range(1, comps):
                        total = total + speeds[d][k] * own[d][k]
                        total = total - now[d][k] * slopes[d][c][k]
                    adj[k, pl.ds(c * cols + x * sy, sy), :] = now[c][k] + HALF * total

    def triples(packed, side):
        width = sy if side < 2 else sx
        wide = unpack(packed, packed.shape[0] // halves)
        return [
            [split(wide[i + c * width : i + (c + 1) * width]) for c in range(comps)]
            for i in range(0, wide.shape[0], comps * width)
        ]

    def fix(s, side, far, far_speed):
        sign = -HALF if side % 2 == 0 else HALF
        across = side // 2
        rows = edge(0, side, 0)
        for k in range(halves):
            at = lambda view, c: view[k, edge(c, side, 0), :]
            carrier = sign * at(vel.at[s], across)
            for c in range(comps):
                new = at(adj, c) + carrier * far[c][k]
                if c == across:
                    total = at(solved, 0) * far_speed[0][k]
                    for d in range(1, comps):
                        total = total + at(solved, d) * far_speed[d][k]
                    new = new - sign * total
                adj[k, edge(c, side, 0), :] = new

    def outside(r, side, far, far_speed, corners):
        across, along = side // 2, 1 - side // 2
        ends = (2 * (side % 2), 2 * (side % 2) + 1) if across == 0 else (side % 2, 2 + side % 2)

        def normal(inner, outer):
            return [(i - o) if side % 2 == 0 else (o - i) for i, o in zip(inner, outer)]

        def diffs(c, view, strip, base):
            mid, outer = strip[0][c], strip[1][c]
            slopes = [None] * 3
            slopes[across] = normal(split(take(view, c, side)), outer)
            row = base + c
            slopes[along] = [
                row_diff(
                    mid[k],
                    corners[ends[0]][k][row : row + 1],
                    corners[ends[1]][k][row : row + 1],
                )
                for k in range(halves)
            ]
            slopes[2] = depth_diff(mid)
            return slopes

        own = [diffs(c, solved, far, 0) for c in range(comps)]
        speed = [diffs(c, vel.at[2 * r], far_speed, comps) for c in range(comps)]
        news = []
        for c in range(comps):
            tiles = []
            for k in range(halves):
                total = far_speed[0][0][k] * own[c][0][k] - far[0][0][k] * speed[0][c][k]
                for d in range(1, comps):
                    total = total + far_speed[0][d][k] * own[c][d][k]
                    total = total - far[0][d][k] * speed[d][c][k]
                tiles.append(far[0][c][k] + HALF * total)
            news.append(jnp.concatenate(tiles, axis=1))
        return news

    rows = lax.broadcasted_iota(jnp.int32, (2 * slots, cols), 0)
    places = lax.broadcasted_iota(jnp.int32, (2 * slots, cols), 1)
    lanes = got.shape[-1]
    span = slots * points
    slot_row = lax.broadcasted_iota(jnp.int32, (slots, span), 0) * points
    slot_col = lax.broadcasted_iota(jnp.int32, (slots, span), 1)
    inside = (slot_col >= slot_row) & (slot_col < slot_row + points)

    def look(sources):
        vectors = []
        for source in sources:
            found = jnp.dot(pick[...], source, preferred_element_type=F32)
            vectors.append(jnp.concatenate([found[:slots], found[slots:]], axis=1))
        stacked = vectors[0] if len(vectors) == 1 else jnp.concatenate(vectors, axis=0)
        return lax.dot_general(
            stacked.astype(BF16), filters[...], (((1,), (1,)), ((), ())), preferred_element_type=F32
        )

    loads[halves].wait()
    whole = inverse[...]
    high = whole.astype(BF16)
    inv_hi[...] = high
    inv_lo[...] = (whole - high.astype(F32)).astype(BF16)
    for load in loads[:halves]:
        load.wait()
    write(solved, everything, product(read(adj, everything)))
    loads[halves + 1].wait()
    loads[halves + 2].wait()
    stage_speed(0)
    stage_solved(0)

    pl.semaphore_wait(barrier, count - 1)
    for k in range(4):
        solved_copy(0, k).start()
        corner_copy(0, k).start()
        speed_copy(0, k).start()
    for k in range(4):
        later_copy(0, k).start()

    for load in loads[halves + 3 :]:
        load.wait()
    wanted = jnp.zeros((2 * slots, cols), jnp.int32)
    for j in range(slots):
        first = 2 * tile_s[0, 0, j]
        wanted = jnp.where(rows == j, first, wanted)
        wanted = jnp.where(rows == slots + j, first + 1, wanted)
    pick[...] = jnp.where(wanted == places, 1.0, 0.0).astype(BF16)
    slot_rows = lax.broadcasted_iota(jnp.int32, (slots, lanes), 0)
    lane = lax.broadcasted_iota(jnp.int32, (slots, lanes), 1)
    named = jnp.full((slots, lanes), turbines, jnp.int32)
    for j in range(slots):
        named = jnp.where(slot_rows == j, turbine_s[0, 0, j], named)
    live[...] = jnp.where((named == lane) & (lane < turbines), 1.0, 0.0)
    lane_row = lax.broadcasted_iota(jnp.int32, (1, lanes), 1)
    owners = jnp.full((1, lanes), -1, jnp.int32)
    for k in range(turbines):
        owners = jnp.where(lane_row == k, owner_s[k], owners)
    mine[...] = jnp.where(owners == me, 1.0, 0.0)
    history[...] = jnp.zeros_like(history)
    weight[...] = jnp.zeros_like(weight)
    terms[...] = jnp.zeros_like(terms)

    def pair(r, carry):
        first, second = 2 * r, 2 * r + 1

        @pl.when(r < steps // 2 - 1)
        def _():
            stage_speed(r + 1)
            for side in range(4):
                speed_copy(r + 1, side).start()
            for side in range(4):
                later_copy(r + 1, side).start()

        local(first)
        sources = [history[i] for i in range(2)]
        sources += [read(vel.at[s], pl.ds(0, cols)).astype(BF16) for s in (first, second)]
        seen = look(sources)
        parts = [seen[i * slots : (i + 1) * slots] for i in range(4)]
        terms[...] += weight[0] * parts[0] + weight[1] * parts[1]
        for i in range(2):
            weight[i] = jnp.where(inside, parts[2 + i] * parts[2 + i], 0.0) * (1.0 / points)

        for k in range(4):
            speed_copy(r, k ^ 1).wait_recv()
            corner_copy(r, k ^ 3).wait_recv()
            solved_copy(r, k ^ 1).wait_recv()
        corners = [split_corner(recv_c[r, q]) for q in range(4)]
        ring = []
        for side in range(4):
            far = triples(recv_s[r, side], side)
            far_speed = triples(recv_v[r, side], side)
            fix(first, side, far[0], far_speed[0])
            ring += outside(r, side, far, far_speed, corners)
        history[0] = read(adj, pl.ds(0, cols)).astype(BF16)
        outer = product(jnp.concatenate(ring, axis=0))
        write(solved, everything, product(read(adj, everything)))

        local(second)
        start = 0
        for side in range(4):
            later_copy(r, side ^ 1).wait_recv()
            width = sy if side < 2 else sx
            far = [split(outer[start + c * width : start + (c + 1) * width]) for c in range(comps)]
            start += comps * width
            fix(second, side, far, triples(recv_w[r, side], side)[0])
        history[1] = read(adj, pl.ds(0, cols)).astype(BF16)

        @pl.when(r < steps // 2 - 1)
        def _():
            write(solved, everything, product(read(adj, everything)))
            stage_solved(r + 1)
            for k in range(4):
                solved_copy(r + 1, k).start()
                corner_copy(r + 1, k).start()

        return carry

    lax.fori_loop(0, steps // 2, pair, 0)

    seen = look([history[i] for i in range(2)])
    total = terms[...] + weight[0] * seen[:slots] + weight[1] * seen[slots:]
    term = jnp.sum(total, axis=1, keepdims=True)
    part[...] = jnp.sum(live[...] * term, axis=0, keepdims=True)

    def share(k):
        return pltpu.make_async_remote_copy(
            src_ref=part, dst_ref=got.at[k - 1], send_sem=st_sem, recv_sem=rt_sem,
            device_id=peer(k), device_id_type=MESH,
        )

    others(lambda k: share(k).start())
    out_ref[...] = read(adj, everything)

    def drain(r, c):
        for k in range(4):
            speed_copy(r, k).wait_send()
            later_copy(r, k).wait_send()
            solved_copy(r, k).wait_send()
            corner_copy(r, k).wait_send()
        return c

    lax.fori_loop(0, steps // 2, drain, 0)
    pltpu.make_async_copy(got, got, st_sem).wait()
    pltpu.make_async_copy(got, got, rt_sem).wait()
    summed = part[...] + jnp.sum(got[...], axis=0)
    grad_ref[...] = jnp.where(mine[...] > 0.0, summed, 0.0)[:, :turbines].reshape(grad_ref.shape)


def hand_over(parts, chunk, final_in, grad_in, final_out, grad_out, sem):
    moves = [pltpu.make_async_copy(grad_in, grad_out, sem.at[parts])]
    for k in range(parts):
        rows = pl.ds(k * chunk, chunk)
        moves.append(pltpu.make_async_copy(final_in.at[rows], final_out.at[rows], sem.at[k]))
    for move in moves:
        move.start()
    for move in moves:
        move.wait()


def body(sizes, adjoint_init, saved_states, step_index, vertical_inverse, disk_filter,
         pair_turbine, pair_tile, turbine_owner):
    ngx, ngy = sizes
    comps, sx, sy, levels = adjoint_init.shape
    saved = saved_states.shape[0]
    steps = step_index.shape[0]
    slots, points, cells = disk_filter.shape[2:]
    turbines = turbine_owner.shape[0]
    rows = comps * sx * sy
    lanes = -(-turbines // 128) * 128
    strip = comps * max(sx, sy) * levels // 128
    halves = levels // 128
    rounds = steps // 2
    count = ngx * ngy
    assert steps % 2 == 0 and sx == sy
    dims = (ngx, ngy, comps, sx, sy, steps, slots, points, turbines)
    anywhere = pl.BlockSpec(memory_space=pl.ANY)
    halo = lambda rows: pltpu.VMEM((rounds, 4, rows, 128), BF16)
    dma = pltpu.SemaphoreType.DMA
    final, grad = pl.pallas_call(
        functools.partial(kernel, dims),
        out_shape=(
            pltpu.VMEM((rows, levels), F32),
            pltpu.VMEM((1, 1, turbines), F32),
        ),
        in_specs=[pl.BlockSpec(memory_space=pltpu.HBM)] * 8,
        out_specs=(pl.BlockSpec(memory_space=pltpu.VMEM),) * 2,
        scratch_shapes=[
            pltpu.VMEM((halves, rows, 128), F32),
            pltpu.VMEM((saved, rows, levels), BF16),
            pltpu.SMEM(step_index.shape, jnp.int32),
            pltpu.VMEM((levels, levels), F32),
            pltpu.VMEM((slots * points, cells), BF16),
            pltpu.SMEM(pair_turbine.shape, jnp.int32),
            pltpu.SMEM(pair_tile.shape, jnp.int32),
            pltpu.SMEM(turbine_owner.shape, jnp.int32),
            pltpu.VMEM((levels, levels), BF16),
            pltpu.VMEM((levels, levels), BF16),
            pltpu.VMEM((halves, rows, 128), F32),
            pltpu.VMEM((steps, halves, rows, 128), F32),
            pltpu.VMEM((2, sx * sy, levels), BF16),
            pltpu.VMEM((2 * slots, sx * sy), BF16),
            pltpu.VMEM((slots, lanes), F32),
            pltpu.VMEM((1, lanes), F32),
            pltpu.VMEM((2, slots, slots * points), F32),
            pltpu.VMEM((slots, slots * points), F32),
            halo(2 * strip), halo(2 * strip), halo(strip), halo(strip), halo(2 * strip), halo(2 * strip),
            halo(8 * halves), halo(8 * halves),
            pltpu.VMEM((1, lanes), F32),
            pltpu.VMEM((count - 1, 1, lanes), F32),
            dma((7 + halves,)),
            *[dma((rounds, 4))] * 8,
            dma, dma,
        ],
        compiler_params=pltpu.CompilerParams(
            collective_id=0, has_side_effects=True, vmem_limit_bytes=60 * 1024 * 1024
        ),
        name="sweep",
    )(
        adjoint_init.reshape(rows, levels),
        saved_states.reshape(saved, rows, levels),
        step_index,
        vertical_inverse,
        disk_filter.reshape(slots * points, cells),
        pair_turbine,
        pair_tile,
        turbine_owner,
    )
    chunk = rows // comps
    final, grad = pl.pallas_call(
        functools.partial(hand_over, comps, chunk),
        out_shape=(
            jax.ShapeDtypeStruct((rows, levels), F32),
            jax.ShapeDtypeStruct((1, 1, turbines), F32),
        ),
        in_specs=[anywhere] * 2,
        out_specs=(anywhere, anywhere),
        scratch_shapes=[dma((comps + 1,))],
        compiler_params=pltpu.CompilerParams(vmem_limit_bytes=1024 * 1024),
        name="hand_over",
    )(final, grad)
    return final.reshape(adjoint_init.shape), grad


def solution(mesh):
    placed = (
        P(None, "gx", "gy", None),
        P(None, None, "gx", "gy", None),
        P(),
        P(),
        P("gx", "gy", None, None, None),
        P("gx", "gy", None),
        P("gx", "gy", None),
        P(),
    )
    return jax.shard_map(
        functools.partial(body, (mesh.shape["gx"], mesh.shape["gy"])),
        mesh=mesh,
        in_specs=placed,
        out_specs=(P(None, "gx", "gy", None), P("gx", "gy", None)),
        check_vma=False,
    )
```

```python
import functools

import jax
import jax.numpy as jnp
from jax import lax
from jax.experimental import pallas as pl
from jax.experimental.pallas import tpu as pltpu
from jax.sharding import PartitionSpec as P

COURANT = 0.2
HALF = 0.5 * COURANT
MESH = pl.DeviceIdType.MESH
F32 = jnp.float32
BF16 = jnp.bfloat16


def pack(rows):
    parts = [rows[:, k : k + 128] for k in range(0, rows.shape[1], 128)]
    return jnp.concatenate(parts, axis=0).astype(BF16)


def unpack(packed, count):
    wide = packed.astype(F32)
    return jnp.concatenate(
        [wide[k : k + count] for k in range(0, wide.shape[0], count)], axis=1
    )


def read(view, rows):
    return jnp.concatenate([view[k, rows, :] for k in range(view.shape[0])], axis=1)


def write(view, rows, value):
    for k in range(view.shape[0]):
        view[k, rows, :] = value[:, 128 * k : 128 * (k + 1)]


def row_diff(tile, low=0.0, high=0.0):
    size = tile.shape[0]
    place = lax.broadcasted_iota(jnp.int32, tile.shape, 0)
    above = jnp.where(place == size - 1, high, pltpu.roll(tile, size - 1, 0))
    below = jnp.where(place == 0, low, pltpu.roll(tile, 1, 0))
    return above - below


def split(wide):
    return [wide[:, k : k + 128] for k in range(0, wide.shape[1], 128)]


def depth_diff(tiles):
    place = lax.broadcasted_iota(jnp.int32, tiles[0].shape, 1)
    ups = [pltpu.roll(tile, 127, 1) for tile in tiles] + [0.0]
    downs = [0.0] + [pltpu.roll(tile, 1, 1) for tile in tiles]
    return [
        jnp.where(place == 127, ups[k + 1], ups[k]) - jnp.where(place == 0, downs[k], downs[k + 1])
        for k in range(len(tiles))
    ]


def kernel(
    dims,
    init_hbm, states_hbm, index_hbm, inverse_hbm, filter_hbm, turbine_hbm, tile_hbm, owner_hbm,
    out_ref, grad_ref,
    adj, states, index_s, inverse, filters, turbine_s, tile_s, owner_s,
    inv_hi, inv_lo, solved, vel, slopes_at, history, pick, live, mine, weight, terms,
    send_v, recv_v, send_w, recv_w, send_s, recv_s, send_c, recv_c,
    part, got,
    load_sem, sv_sem, rv_sem, sw_sem, rw_sem, ss_sem, rs_sem, sc_sem, rc_sem, st_sem, rt_sem,
):
    ngx, ngy, comps, sx, sy, steps, slots, points, turbines = dims
    cols = sx * sy
    halves = adj.shape[0]
    levels = 128 * halves
    everything = pl.ds(0, comps * cols)
    gx, gy = lax.axis_index("gx"), lax.axis_index("gy")

    loads = [
        pltpu.make_async_copy(src, dst, load_sem.at[k])
        for k, (src, dst) in enumerate((
            *((init_hbm.at[:, pl.ds(128 * k, 128)], adj.at[k]) for k in range(halves)),
            (inverse_hbm, inverse), (index_hbm, index_s), (states_hbm, states),
            (turbine_hbm, turbine_s), (tile_hbm, tile_s), (owner_hbm, owner_s), (filter_hbm, filters),
        ))
    ]
    for load in loads:
        load.start()

    barrier = pltpu.get_barrier_semaphore()

    count = ngx * ngy
    me = gx * ngy + gy

    def peer(k):
        if isinstance(k, int):
            x, y = gx + k // ngy, gy + k % ngy
            return (jnp.where(x >= ngx, x - ngx, x), jnp.where(y >= ngy, y - ngy, y))
        return (lax.rem(gx + k // ngy, ngx), lax.rem(gy + lax.rem(k, ngy), ngy))

    def others(act):
        if count <= 64:
            for k in range(1, count):
                act(k)
        else:
            def one(k, c):
                act(k)
                return c
            lax.fori_loop(1, count, one, 0)

    others(lambda k: pl.semaphore_signal(barrier, inc=1, device_id=peer(k), device_id_type=MESH))

    beside_x = (lax.rem(gx + ngx - 1, ngx), lax.rem(gx + 1, ngx))
    beside_y = (lax.rem(gy + ngy - 1, ngy), lax.rem(gy + 1, ngy))
    beside = [(x, gy) for x in beside_x] + [(gx, y) for y in beside_y]
    aslant = [(x, y) for x in beside_x for y in beside_y]

    def edge(c, side, depth):
        base = c * cols
        if side == 0:
            return pl.ds(base + depth * sy, sy)
        if side == 1:
            return pl.ds(base + cols - (depth + 1) * sy, sy)
        return pl.ds(base + (depth if side == 2 else sy - 1 - depth), sx, stride=sy)

    def take(view, c, side, depth=0):
        return read(view, edge(c, side, depth))

    def put(view, c, side, value):
        write(view, edge(c, side, 0), value)

    def strips(view, side, depths):
        return [take(view, c, side, depth) for depth in depths for c in range(comps)]

    def stage_first(r):
        write(vel.at[2 * r], everything, states[index_s[2 * r]].astype(F32))
        for side in range(4):
            send_v[r, side] = pack(jnp.concatenate(strips(vel.at[2 * r], side, (0, 1)), axis=0))

    def stage_second(r):
        write(vel.at[2 * r + 1], everything, states[index_s[2 * r + 1]].astype(F32))
        for side in range(4):
            send_w[r, side] = pack(jnp.concatenate(strips(vel.at[2 * r + 1], side, (0,)), axis=0))

    def stage_solved(r):
        for side in range(4):
            send_s[r, side] = pack(jnp.concatenate(strips(solved, side, (0, 1)), axis=0))
        place = lax.broadcasted_iota(jnp.int32, (8, 128), 0)
        for q in range(4):
            cell = (q // 2) * (sx - 1) * sy + (q % 2) * (sy - 1)
            tiles = []
            for k in range(halves):
                tile = jnp.zeros((8, 128), F32)
                for c in range(comps):
                    row = pl.ds(c * cols + cell, 1)
                    tile = jnp.where(place == c, solved[k, row, :], tile)
                    tile = jnp.where(place == comps + c, vel[2 * r, k, row, :], tile)
                tiles.append(tile)
            send_c[r, q] = jnp.concatenate(tiles, axis=0).astype(BF16)

    def remote(staging, landing, ssem, rsem, r, k, flip, where):
        return pltpu.make_async_remote_copy(
            src_ref=staging.at[r, k],
            dst_ref=landing.at[r, k ^ flip],
            send_sem=ssem.at[r, k],
            recv_sem=rsem.at[r, k ^ flip],
            device_id=where[k],
            device_id_type=MESH,
        )

    def speed_copy(r, side):
        return remote(send_v, recv_v, sv_sem, rv_sem, r, side, 1, beside)

    def later_copy(r, side):
        return remote(send_w, recv_w, sw_sem, rw_sem, r, side, 1, beside)

    def solved_copy(r, side):
        return remote(send_s, recv_s, ss_sem, rs_sem, r, side, 1, beside)

    def corner_copy(r, q):
        return remote(send_c, recv_c, sc_sem, rc_sem, r, q, 3, aslant)

    def split_corner(packed):
        wide = packed.astype(F32)
        return [wide[8 * k : 8 * (k + 1)] for k in range(halves)]

    def product(value):
        hi = value.astype(BF16)
        lo = (value - hi.astype(F32)).astype(BF16)
        dot = functools.partial(jnp.dot, preferred_element_type=F32)
        return dot(hi, inv_hi[...]) + (dot(hi, inv_lo[...]) + dot(lo, inv_hi[...]))

    def field(view, c, x):
        if x < 0 or x >= sx:
            return [jnp.zeros((sy, 128), F32)] * halves
        return [view[k, pl.ds(c * cols + x * sy, sy), :] for k in range(halves)]

    def diffs(view, c, x):
        mid = field(view, c, x)
        low, high = field(view, c, x - 1), field(view, c, x + 1)
        return (
            [high[k] - low[k] for k in range(halves)],
            [row_diff(tile) for tile in mid],
            depth_diff(mid),
        )

    def make_slopes(s):
        for x in range(sx):
            for c in range(comps):
                made = diffs(vel.at[s], c, x)
                for d in range(3):
                    for k in range(halves):
                        slopes_at[3 * c + d, k, pl.ds(x * sy, sy), :] = made[d][k]

    def local(s, ready):
        speed = vel.at[s]

        def speed_slopes(c, x):
            if not ready:
                return diffs(speed, c, x)
            rows = pl.ds(x * sy, sy)
            return [[slopes_at[3 * c + d, k, rows, :] for k in range(halves)] for d in range(3)]

        for x in range(sx):
            speeds = [field(speed, c, x) for c in range(comps)]
            now = [field(solved, c, x) for c in range(comps)]
            slopes = [speed_slopes(c, x) for c in range(comps)]
            for c in range(comps):
                own = diffs(solved, c, x)
                for k in range(halves):
                    total = speeds[0][k] * own[0][k] - now[0][k] * slopes[0][c][k]
                    for d in range(1, comps):
                        total = total + speeds[d][k] * own[d][k]
                        total = total - now[d][k] * slopes[d][c][k]
                    adj[k, pl.ds(c * cols + x * sy, sy), :] = now[c][k] + HALF * total

    def triples(packed, side):
        width = sy if side < 2 else sx
        wide = unpack(packed, packed.shape[0] // halves)
        return [
            [split(wide[i + c * width : i + (c + 1) * width]) for c in range(comps)]
            for i in range(0, wide.shape[0], comps * width)
        ]

    def fix(s, side, far, far_speed):
        sign = -HALF if side % 2 == 0 else HALF
        across = side // 2
        rows = edge(0, side, 0)
        for k in range(halves):
            at = lambda view, c: view[k, edge(c, side, 0), :]
            carrier = sign * at(vel.at[s], across)
            for c in range(comps):
                new = at(adj, c) + carrier * far[c][k]
                if c == across:
                    total = at(solved, 0) * far_speed[0][k]
                    for d in range(1, comps):
                        total = total + at(solved, d) * far_speed[d][k]
                    new = new - sign * total
                adj[k, edge(c, side, 0), :] = new

    def outside(r, side, far, far_speed, corners):
        across, along = side // 2, 1 - side // 2
        ends = (2 * (side % 2), 2 * (side % 2) + 1) if across == 0 else (side % 2, 2 + side % 2)

        def normal(inner, outer):
            return [(i - o) if side % 2 == 0 else (o - i) for i, o in zip(inner, outer)]

        def diffs(c, view, strip, base):
            mid, outer = strip[0][c], strip[1][c]
            slopes = [None] * 3
            slopes[across] = normal(split(take(view, c, side)), outer)
            row = base + c
            slopes[along] = [
                row_diff(
                    mid[k],
                    corners[ends[0]][k][row : row + 1],
                    corners[ends[1]][k][row : row + 1],
                )
                for k in range(halves)
            ]
            slopes[2] = depth_diff(mid)
            return slopes

        own = [diffs(c, solved, far, 0) for c in range(comps)]
        speed = [diffs(c, vel.at[2 * r], far_speed, comps) for c in range(comps)]
        news = []
        for c in range(comps):
            tiles = []
            for k in range(halves):
                total = far_speed[0][0][k] * own[c][0][k] - far[0][0][k] * speed[0][c][k]
                for d in range(1, comps):
                    total = total + far_speed[0][d][k] * own[c][d][k]
                    total = total - far[0][d][k] * speed[d][c][k]
                tiles.append(far[0][c][k] + HALF * total)
            news.append(jnp.concatenate(tiles, axis=1))
        return news

    rows = lax.broadcasted_iota(jnp.int32, (2 * slots, cols), 0)
    places = lax.broadcasted_iota(jnp.int32, (2 * slots, cols), 1)
    lanes = got.shape[-1]
    span = slots * points
    slot_row = lax.broadcasted_iota(jnp.int32, (slots, span), 0) * points
    slot_col = lax.broadcasted_iota(jnp.int32, (slots, span), 1)
    inside = (slot_col >= slot_row) & (slot_col < slot_row + points)

    def look(sources):
        vectors = []
        for source in sources:
            found = jnp.dot(pick[...], source, preferred_element_type=F32)
            vectors.append(jnp.concatenate([found[:slots], found[slots:]], axis=1))
        stacked = vectors[0] if len(vectors) == 1 else jnp.concatenate(vectors, axis=0)
        return lax.dot_general(
            stacked.astype(BF16), filters[...], (((1,), (1,)), ((), ())), preferred_element_type=F32
        )

    loads[halves].wait()
    whole = inverse[...]
    high = whole.astype(BF16)
    inv_hi[...] = high
    inv_lo[...] = (whole - high.astype(F32)).astype(BF16)
    for load in loads[:halves]:
        load.wait()
    loads[halves + 1].wait()
    loads[halves + 2].wait()
    stage_first(0)
    pl.semaphore_wait(barrier, count - 1)
    for k in range(4):
        speed_copy(0, k).start()
    write(solved, everything, product(read(adj, everything)))
    stage_solved(0)
    for k in range(4):
        solved_copy(0, k).start()
        corner_copy(0, k).start()
    stage_second(0)
    for k in range(4):
        later_copy(0, k).start()

    for load in loads[halves + 3 :]:
        load.wait()
    wanted = jnp.zeros((2 * slots, cols), jnp.int32)
    for j in range(slots):
        first = 2 * tile_s[0, 0, j]
        wanted = jnp.where(rows == j, first, wanted)
        wanted = jnp.where(rows == slots + j, first + 1, wanted)
    pick[...] = jnp.where(wanted == places, 1.0, 0.0).astype(BF16)
    slot_rows = lax.broadcasted_iota(jnp.int32, (slots, lanes), 0)
    lane = lax.broadcasted_iota(jnp.int32, (slots, lanes), 1)
    named = jnp.full((slots, lanes), turbines, jnp.int32)
    for j in range(slots):
        named = jnp.where(slot_rows == j, turbine_s[0, 0, j], named)
    live[...] = jnp.where((named == lane) & (lane < turbines), 1.0, 0.0)
    lane_row = lax.broadcasted_iota(jnp.int32, (1, lanes), 1)
    owners = jnp.full((1, lanes), -1, jnp.int32)
    for k in range(turbines):
        owners = jnp.where(lane_row == k, owner_s[k], owners)
    mine[...] = jnp.where(owners == me, 1.0, 0.0)
    history[...] = jnp.zeros_like(history)
    weight[...] = jnp.zeros_like(weight)
    terms[...] = jnp.zeros_like(terms)

    def pair(r, carry):
        first, second = 2 * r, 2 * r + 1

        @pl.when(r < steps // 2 - 1)
        def _():
            stage_first(r + 1)
            stage_second(r + 1)
            for side in range(4):
                speed_copy(r + 1, side).start()
            for side in range(4):
                later_copy(r + 1, side).start()

        local(first, False)
        make_slopes(second)
        sources = [history[i] for i in range(2)]
        sources += [read(vel.at[s], pl.ds(0, cols)).astype(BF16) for s in (first, second)]
        seen = look(sources)
        parts = [seen[i * slots : (i + 1) * slots] for i in range(4)]
        terms[...] += weight[0] * parts[0] + weight[1] * parts[1]
        for i in range(2):
            weight[i] = jnp.where(inside, parts[2 + i] * parts[2 + i], 0.0) * (1.0 / points)

        for k in range(4):
            speed_copy(r, k ^ 1).wait_recv()
            corner_copy(r, k ^ 3).wait_recv()
            solved_copy(r, k ^ 1).wait_recv()
        corners = [split_corner(recv_c[r, q]) for q in range(4)]
        ring = []
        for side in range(4):
            far = triples(recv_s[r, side], side)
            far_speed = triples(recv_v[r, side], side)
            fix(first, side, far[0], far_speed[0])
            ring += outside(r, side, far, far_speed, corners)
        history[0] = read(adj, pl.ds(0, cols)).astype(BF16)
        outer = product(jnp.concatenate(ring, axis=0))
        write(solved, everything, product(read(adj, everything)))

        local(second, True)
        start = 0
        for side in range(4):
            later_copy(r, side ^ 1).wait_recv()
            width = sy if side < 2 else sx
            far = [split(outer[start + c * width : start + (c + 1) * width]) for c in range(comps)]
            start += comps * width
            fix(second, side, far, triples(recv_w[r, side], side)[0])
        history[1] = read(adj, pl.ds(0, cols)).astype(BF16)

        @pl.when(r < steps // 2 - 1)
        def _():
            write(solved, everything, product(read(adj, everything)))
            stage_solved(r + 1)
            for k in range(4):
                solved_copy(r + 1, k).start()
                corner_copy(r + 1, k).start()

        return carry

    lax.fori_loop(0, steps // 2, pair, 0)

    seen = look([history[i] for i in range(2)])
    total = terms[...] + weight[0] * seen[:slots] + weight[1] * seen[slots:]
    term = jnp.sum(total, axis=1, keepdims=True)
    part[...] = jnp.sum(live[...] * term, axis=0, keepdims=True)

    def share(k):
        return pltpu.make_async_remote_copy(
            src_ref=part, dst_ref=got.at[k - 1], send_sem=st_sem, recv_sem=rt_sem,
            device_id=peer(k), device_id_type=MESH,
        )

    others(lambda k: share(k).start())
    out_ref[...] = read(adj, everything)

    def drain(r, c):
        for k in range(4):
            speed_copy(r, k).wait_send()
            later_copy(r, k).wait_send()
            solved_copy(r, k).wait_send()
            corner_copy(r, k).wait_send()
        return c

    lax.fori_loop(0, steps // 2, drain, 0)
    pltpu.make_async_copy(got, got, st_sem).wait()
    pltpu.make_async_copy(got, got, rt_sem).wait()
    summed = part[...] + jnp.sum(got[...], axis=0)
    grad_ref[...] = jnp.where(mine[...] > 0.0, summed, 0.0)[:, :turbines].reshape(grad_ref.shape)


def hand_over(parts, chunk, final_in, grad_in, final_out, grad_out, sem):
    moves = [pltpu.make_async_copy(grad_in, grad_out, sem.at[parts])]
    for k in range(parts):
        rows = pl.ds(k * chunk, chunk)
        moves.append(pltpu.make_async_copy(final_in.at[rows], final_out.at[rows], sem.at[k]))
    for move in moves:
        move.start()
    for move in moves:
        move.wait()


def body(sizes, adjoint_init, saved_states, step_index, vertical_inverse, disk_filter,
         pair_turbine, pair_tile, turbine_owner):
    ngx, ngy = sizes
    comps, sx, sy, levels = adjoint_init.shape
    saved = saved_states.shape[0]
    steps = step_index.shape[0]
    slots, points, cells = disk_filter.shape[2:]
    turbines = turbine_owner.shape[0]
    rows = comps * sx * sy
    lanes = -(-turbines // 128) * 128
    strip = comps * max(sx, sy) * levels // 128
    halves = levels // 128
    rounds = steps // 2
    count = ngx * ngy
    assert steps % 2 == 0 and sx == sy
    dims = (ngx, ngy, comps, sx, sy, steps, slots, points, turbines)
    anywhere = pl.BlockSpec(memory_space=pl.ANY)
    halo = lambda rows: pltpu.VMEM((rounds, 4, rows, 128), BF16)
    dma = pltpu.SemaphoreType.DMA
    final, grad = pl.pallas_call(
        functools.partial(kernel, dims),
        out_shape=(
            pltpu.VMEM((rows, levels), F32),
            pltpu.VMEM((1, 1, turbines), F32),
        ),
        in_specs=[pl.BlockSpec(memory_space=pltpu.HBM)] * 8,
        out_specs=(pl.BlockSpec(memory_space=pltpu.VMEM),) * 2,
        scratch_shapes=[
            pltpu.VMEM((halves, rows, 128), F32),
            pltpu.VMEM((saved, rows, levels), BF16),
            pltpu.SMEM(step_index.shape, jnp.int32),
            pltpu.VMEM((levels, levels), F32),
            pltpu.VMEM((slots * points, cells), BF16),
            pltpu.SMEM(pair_turbine.shape, jnp.int32),
            pltpu.SMEM(pair_tile.shape, jnp.int32),
            pltpu.SMEM(turbine_owner.shape, jnp.int32),
            pltpu.VMEM((levels, levels), BF16),
            pltpu.VMEM((levels, levels), BF16),
            pltpu.VMEM((halves, rows, 128), F32),
            pltpu.VMEM((steps, halves, rows, 128), F32),
            pltpu.VMEM((3 * comps, halves, sx * sy, 128), F32),
            pltpu.VMEM((2, sx * sy, levels), BF16),
            pltpu.VMEM((2 * slots, sx * sy), BF16),
            pltpu.VMEM((slots, lanes), F32),
            pltpu.VMEM((1, lanes), F32),
            pltpu.VMEM((2, slots, slots * points), F32),
            pltpu.VMEM((slots, slots * points), F32),
            halo(2 * strip), halo(2 * strip), halo(strip), halo(strip), halo(2 * strip), halo(2 * strip),
            halo(8 * halves), halo(8 * halves),
            pltpu.VMEM((1, lanes), F32),
            pltpu.VMEM((count - 1, 1, lanes), F32),
            dma((7 + halves,)),
            *[dma((rounds, 4))] * 8,
            dma, dma,
        ],
        compiler_params=pltpu.CompilerParams(
            collective_id=0, has_side_effects=True, vmem_limit_bytes=60 * 1024 * 1024
        ),
        name="sweep",
    )(
        adjoint_init.reshape(rows, levels),
        saved_states.reshape(saved, rows, levels),
        step_index,
        vertical_inverse,
        disk_filter.reshape(slots * points, cells),
        pair_turbine,
        pair_tile,
        turbine_owner,
    )
    chunk = rows // comps
    final, grad = pl.pallas_call(
        functools.partial(hand_over, comps, chunk),
        out_shape=(
            jax.ShapeDtypeStruct((rows, levels), F32),
            jax.ShapeDtypeStruct((1, 1, turbines), F32),
        ),
        in_specs=[anywhere] * 2,
        out_specs=(anywhere, anywhere),
        scratch_shapes=[dma((comps + 1,))],
        compiler_params=pltpu.CompilerParams(vmem_limit_bytes=1024 * 1024),
        name="hand_over",
    )(final, grad)
    return final.reshape(adjoint_init.shape), grad


def solution(mesh):
    placed = (
        P(None, "gx", "gy", None),
        P(None, None, "gx", "gy", None),
        P(),
        P(),
        P("gx", "gy", None, None, None),
        P("gx", "gy", None),
        P("gx", "gy", None),
        P(),
    )
    return jax.shard_map(
        functools.partial(body, (mesh.shape["gx"], mesh.shape["gy"])),
        mesh=mesh,
        in_specs=placed,
        out_specs=(P(None, "gx", "gy", None), P("gx", "gy", None)),
        check_vma=False,
    )
```

```python
import functools

import jax
import jax.numpy as jnp
from jax import lax
from jax.experimental import pallas as pl
from jax.experimental.pallas import tpu as pltpu
from jax.sharding import PartitionSpec as P

COURANT = 0.2
HALF = 0.5 * COURANT
MESH = pl.DeviceIdType.MESH
F32 = jnp.float32
BF16 = jnp.bfloat16


def pack(rows):
    parts = [rows[:, k : k + 128] for k in range(0, rows.shape[1], 128)]
    return jnp.concatenate(parts, axis=0).astype(BF16)


def unpack(packed, count):
    wide = packed.astype(F32)
    return jnp.concatenate(
        [wide[k : k + count] for k in range(0, wide.shape[0], count)], axis=1
    )


def read(view, rows):
    return jnp.concatenate([view[k, rows, :] for k in range(view.shape[0])], axis=1)


def write(view, rows, value):
    for k in range(view.shape[0]):
        view[k, rows, :] = value[:, 128 * k : 128 * (k + 1)]


def row_diff(tile, low=0.0, high=0.0):
    size = tile.shape[0]
    place = lax.broadcasted_iota(jnp.int32, tile.shape, 0)
    above = jnp.where(place == size - 1, high, pltpu.roll(tile, size - 1, 0))
    below = jnp.where(place == 0, low, pltpu.roll(tile, 1, 0))
    return above - below


def split(wide):
    return [wide[:, k : k + 128] for k in range(0, wide.shape[1], 128)]


def depth_diff(tiles):
    place = lax.broadcasted_iota(jnp.int32, tiles[0].shape, 1)
    ups = [pltpu.roll(tile, 127, 1) for tile in tiles] + [0.0]
    downs = [0.0] + [pltpu.roll(tile, 1, 1) for tile in tiles]
    return [
        jnp.where(place == 127, ups[k + 1], ups[k]) - jnp.where(place == 0, downs[k], downs[k + 1])
        for k in range(len(tiles))
    ]


def kernel(
    dims,
    init_hbm, states_hbm, index_hbm, inverse_hbm, filter_hbm, turbine_hbm, tile_hbm, owner_hbm,
    out_ref, grad_ref,
    adj, states, index_s, inverse, filters, turbine_s, tile_s, owner_s,
    inv_hi, inv_lo, solved, vel, history, pick, live, mine, weight, terms,
    send_v, recv_v, send_w, recv_w, send_s, recv_s, send_c, recv_c,
    part, got,
    load_sem, sv_sem, rv_sem, sw_sem, rw_sem, ss_sem, rs_sem, sc_sem, rc_sem, st_sem, rt_sem,
):
    ngx, ngy, comps, sx, sy, steps, slots, points, turbines = dims
    cols = sx * sy
    halves = adj.shape[0]
    levels = 128 * halves
    everything = pl.ds(0, comps * cols)
    gx, gy = lax.axis_index("gx"), lax.axis_index("gy")

    loads = [
        pltpu.make_async_copy(src, dst, load_sem.at[k])
        for k, (src, dst) in enumerate((
            *((init_hbm.at[:, pl.ds(128 * k, 128)], adj.at[k]) for k in range(halves)),
            (inverse_hbm, inverse), (index_hbm, index_s), (states_hbm, states),
            (turbine_hbm, turbine_s), (tile_hbm, tile_s), (owner_hbm, owner_s), (filter_hbm, filters),
        ))
    ]
    for load in loads:
        load.start()

    barrier = pltpu.get_barrier_semaphore()

    count = ngx * ngy
    me = gx * ngy + gy

    def peer(k):
        if isinstance(k, int):
            x, y = gx + k // ngy, gy + k % ngy
            return (jnp.where(x >= ngx, x - ngx, x), jnp.where(y >= ngy, y - ngy, y))
        return (lax.rem(gx + k // ngy, ngx), lax.rem(gy + lax.rem(k, ngy), ngy))

    def others(act):
        if count <= 64:
            for k in range(1, count):
                act(k)
        else:
            def one(k, c):
                act(k)
                return c
            lax.fori_loop(1, count, one, 0)

    others(lambda k: pl.semaphore_signal(barrier, inc=1, device_id=peer(k), device_id_type=MESH))

    beside_x = (lax.rem(gx + ngx - 1, ngx), lax.rem(gx + 1, ngx))
    beside_y = (lax.rem(gy + ngy - 1, ngy), lax.rem(gy + 1, ngy))
    beside = [(x, gy) for x in beside_x] + [(gx, y) for y in beside_y]
    aslant = [(x, y) for x in beside_x for y in beside_y]

    def edge(c, side, depth):
        base = c * cols
        if side == 0:
            return pl.ds(base + depth * sy, sy)
        if side == 1:
            return pl.ds(base + cols - (depth + 1) * sy, sy)
        return pl.ds(base + (depth if side == 2 else sy - 1 - depth), sx, stride=sy)

    def take(view, c, side, depth=0):
        return read(view, edge(c, side, depth))

    def put(view, c, side, value):
        write(view, edge(c, side, 0), value)

    def strips(view, side, depths):
        return [take(view, c, side, depth) for depth in depths for c in range(comps)]

    def stage_speed(r):
        for s in (2 * r, 2 * r + 1):
            write(vel.at[s], everything, states[index_s[s]].astype(F32))
        for side in range(4):
            send_v[r, side] = pack(jnp.concatenate(strips(vel.at[2 * r], side, (0, 1)), axis=0))
            send_w[r, side] = pack(jnp.concatenate(strips(vel.at[2 * r + 1], side, (0,)), axis=0))

    def stage_solved(r, go):
        for side in range(4):
            send_s[r, side] = pack(jnp.concatenate(strips(solved, side, (0, 1)), axis=0))
            if go:
                solved_copy(r, side).start()
        place = lax.broadcasted_iota(jnp.int32, (8, 128), 0)
        for q in range(4):
            cell = (q // 2) * (sx - 1) * sy + (q % 2) * (sy - 1)
            tiles = []
            for k in range(halves):
                tile = jnp.zeros((8, 128), F32)
                for c in range(comps):
                    row = pl.ds(c * cols + cell, 1)
                    tile = jnp.where(place == c, solved[k, row, :], tile)
                    tile = jnp.where(place == comps + c, vel[2 * r, k, row, :], tile)
                tiles.append(tile)
            send_c[r, q] = jnp.concatenate(tiles, axis=0).astype(BF16)

    def remote(staging, landing, ssem, rsem, r, k, flip, where):
        return pltpu.make_async_remote_copy(
            src_ref=staging.at[r, k],
            dst_ref=landing.at[r, k ^ flip],
            send_sem=ssem.at[r, k],
            recv_sem=rsem.at[r, k ^ flip],
            device_id=where[k],
            device_id_type=MESH,
        )

    def speed_copy(r, side):
        return remote(send_v, recv_v, sv_sem, rv_sem, r, side, 1, beside)

    def later_copy(r, side):
        return remote(send_w, recv_w, sw_sem, rw_sem, r, side, 1, beside)

    def solved_copy(r, side):
        return remote(send_s, recv_s, ss_sem, rs_sem, r, side, 1, beside)

    def corner_copy(r, q):
        return remote(send_c, recv_c, sc_sem, rc_sem, r, q, 3, aslant)

    def split_corner(packed):
        wide = packed.astype(F32)
        return [wide[8 * k : 8 * (k + 1)] for k in range(halves)]

    def product(value):
        hi = value.astype(BF16)
        lo = (value - hi.astype(F32)).astype(BF16)
        dot = functools.partial(jnp.dot, preferred_element_type=F32)
        return dot(hi, inv_hi[...]) + (dot(hi, inv_lo[...]) + dot(lo, inv_hi[...]))

    def local(s):
        def field(view, c, x):
            if x < 0 or x >= sx:
                return [jnp.zeros((sy, 128), F32)] * halves
            return [view[k, pl.ds(c * cols + x * sy, sy), :] for k in range(halves)]

        def diffs(view, c, x):
            mid = field(view, c, x)
            low, high = field(view, c, x - 1), field(view, c, x + 1)
            return (
                [high[k] - low[k] for k in range(halves)],
                [row_diff(tile) for tile in mid],
                depth_diff(mid),
            )

        speed = vel.at[s]
        for x in range(sx):
            speeds = [field(speed, c, x) for c in range(comps)]
            now = [field(solved, c, x) for c in range(comps)]
            slopes = [diffs(speed, c, x) for c in range(comps)]
            for c in range(comps):
                own = diffs(solved, c, x)
                for k in range(halves):
                    total = speeds[0][k] * own[0][k] - now[0][k] * slopes[0][c][k]
                    for d in range(1, comps):
                        total = total + speeds[d][k] * own[d][k]
                        total = total - now[d][k] * slopes[d][c][k]
                    adj[k, pl.ds(c * cols + x * sy, sy), :] = now[c][k] + HALF * total

    def triples(packed, side):
        width = sy if side < 2 else sx
        wide = unpack(packed, packed.shape[0] // halves)
        return [
            [split(wide[i + c * width : i + (c + 1) * width]) for c in range(comps)]
            for i in range(0, wide.shape[0], comps * width)
        ]

    def fix(s, side, far, far_speed):
        sign = -HALF if side % 2 == 0 else HALF
        across = side // 2
        rows = edge(0, side, 0)
        for k in range(halves):
            at = lambda view, c: view[k, edge(c, side, 0), :]
            carrier = sign * at(vel.at[s], across)
            for c in range(comps):
                new = at(adj, c) + carrier * far[c][k]
                if c == across:
                    total = at(solved, 0) * far_speed[0][k]
                    for d in range(1, comps):
                        total = total + at(solved, d) * far_speed[d][k]
                    new = new - sign * total
                adj[k, edge(c, side, 0), :] = new

    def outside(r, side, far, far_speed, corners):
        across, along = side // 2, 1 - side // 2
        ends = (2 * (side % 2), 2 * (side % 2) + 1) if across == 0 else (side % 2, 2 + side % 2)

        def normal(inner, outer):
            return [(i - o) if side % 2 == 0 else (o - i) for i, o in zip(inner, outer)]

        def diffs(c, view, strip, base):
            mid, outer = strip[0][c], strip[1][c]
            slopes = [None] * 3
            slopes[across] = normal(split(take(view, c, side)), outer)
            row = base + c
            slopes[along] = [
                row_diff(
                    mid[k],
                    corners[ends[0]][k][row : row + 1],
                    corners[ends[1]][k][row : row + 1],
                )
                for k in range(halves)
            ]
            slopes[2] = depth_diff(mid)
            return slopes

        own = [diffs(c, solved, far, 0) for c in range(comps)]
        speed = [diffs(c, vel.at[2 * r], far_speed, comps) for c in range(comps)]
        news = []
        for c in range(comps):
            tiles = []
            for k in range(halves):
                total = far_speed[0][0][k] * own[c][0][k] - far[0][0][k] * speed[0][c][k]
                for d in range(1, comps):
                    total = total + far_speed[0][d][k] * own[c][d][k]
                    total = total - far[0][d][k] * speed[d][c][k]
                tiles.append(far[0][c][k] + HALF * total)
            news.append(jnp.concatenate(tiles, axis=1))
        return news

    rows = lax.broadcasted_iota(jnp.int32, (2 * slots, cols), 0)
    places = lax.broadcasted_iota(jnp.int32, (2 * slots, cols), 1)
    lanes = got.shape[-1]
    span = slots * points
    slot_row = lax.broadcasted_iota(jnp.int32, (slots, span), 0) * points
    slot_col = lax.broadcasted_iota(jnp.int32, (slots, span), 1)
    inside = (slot_col >= slot_row) & (slot_col < slot_row + points)

    def look(sources):
        vectors = []
        for source in sources:
            found = jnp.dot(pick[...], source, preferred_element_type=F32)
            vectors.append(jnp.concatenate([found[:slots], found[slots:]], axis=1))
        stacked = vectors[0] if len(vectors) == 1 else jnp.concatenate(vectors, axis=0)
        return lax.dot_general(
            stacked.astype(BF16), filters[...], (((1,), (1,)), ((), ())), preferred_element_type=F32
        )

    loads[halves].wait()
    whole = inverse[...]
    high = whole.astype(BF16)
    inv_hi[...] = high
    inv_lo[...] = (whole - high.astype(F32)).astype(BF16)
    for load in loads[:halves]:
        load.wait()
    write(solved, everything, product(read(adj, everything)))
    loads[halves + 1].wait()
    loads[halves + 2].wait()
    stage_speed(0)
    stage_solved(0, False)

    pl.semaphore_wait(barrier, count - 1)
    for k in range(4):
        solved_copy(0, k).start()
        corner_copy(0, k).start()
        speed_copy(0, k).start()
    for k in range(4):
        later_copy(0, k).start()

    for load in loads[halves + 3 :]:
        load.wait()
    wanted = jnp.zeros((2 * slots, cols), jnp.int32)
    for j in range(slots):
        first = 2 * tile_s[0, 0, j]
        wanted = jnp.where(rows == j, first, wanted)
        wanted = jnp.where(rows == slots + j, first + 1, wanted)
    pick[...] = jnp.where(wanted == places, 1.0, 0.0).astype(BF16)
    slot_rows = lax.broadcasted_iota(jnp.int32, (slots, lanes), 0)
    lane = lax.broadcasted_iota(jnp.int32, (slots, lanes), 1)
    named = jnp.full((slots, lanes), turbines, jnp.int32)
    for j in range(slots):
        named = jnp.where(slot_rows == j, turbine_s[0, 0, j], named)
    live[...] = jnp.where((named == lane) & (lane < turbines), 1.0, 0.0)
    lane_row = lax.broadcasted_iota(jnp.int32, (1, lanes), 1)
    owners = jnp.full((1, lanes), -1, jnp.int32)
    for k in range(turbines):
        owners = jnp.where(lane_row == k, owner_s[k], owners)
    mine[...] = jnp.where(owners == me, 1.0, 0.0)
    history[...] = jnp.zeros_like(history)
    weight[...] = jnp.zeros_like(weight)
    terms[...] = jnp.zeros_like(terms)

    def pair(r, carry):
        first, second = 2 * r, 2 * r + 1

        @pl.when(r < steps // 2 - 1)
        def _():
            stage_speed(r + 1)
            for side in range(4):
                speed_copy(r + 1, side).start()
            for side in range(4):
                later_copy(r + 1, side).start()

        local(first)
        sources = [history[i] for i in range(2)]
        sources += [read(vel.at[s], pl.ds(0, cols)).astype(BF16) for s in (first, second)]
        seen = look(sources)
        parts = [seen[i * slots : (i + 1) * slots] for i in range(4)]
        terms[...] += weight[0] * parts[0] + weight[1] * parts[1]
        for i in range(2):
            weight[i] = jnp.where(inside, parts[2 + i] * parts[2 + i], 0.0) * (1.0 / points)

        for k in range(4):
            speed_copy(r, k ^ 1).wait_recv()
            corner_copy(r, k ^ 3).wait_recv()
            solved_copy(r, k ^ 1).wait_recv()
        corners = [split_corner(recv_c[r, q]) for q in range(4)]
        ring = []
        for side in range(4):
            far = triples(recv_s[r, side], side)
            far_speed = triples(recv_v[r, side], side)
            fix(first, side, far[0], far_speed[0])
            ring += outside(r, side, far, far_speed, corners)
        history[0] = read(adj, pl.ds(0, cols)).astype(BF16)
        outer = product(jnp.concatenate(ring, axis=0))
        write(solved, everything, product(read(adj, everything)))

        local(second)
        start = 0
        for side in range(4):
            later_copy(r, side ^ 1).wait_recv()
            width = sy if side < 2 else sx
            far = [split(outer[start + c * width : start + (c + 1) * width]) for c in range(comps)]
            start += comps * width
            fix(second, side, far, triples(recv_w[r, side], side)[0])
        history[1] = read(adj, pl.ds(0, cols)).astype(BF16)

        @pl.when(r < steps // 2 - 1)
        def _():
            write(solved, everything, product(read(adj, everything)))
            stage_solved(r + 1, True)
            for k in range(4):
                corner_copy(r + 1, k).start()

        return carry

    lax.fori_loop(0, steps // 2, pair, 0)

    seen = look([history[i] for i in range(2)])
    total = terms[...] + weight[0] * seen[:slots] + weight[1] * seen[slots:]
    term = jnp.sum(total, axis=1, keepdims=True)
    part[...] = jnp.sum(live[...] * term, axis=0, keepdims=True)

    def share(k):
        return pltpu.make_async_remote_copy(
            src_ref=part, dst_ref=got.at[k - 1], send_sem=st_sem, recv_sem=rt_sem,
            device_id=peer(k), device_id_type=MESH,
        )

    others(lambda k: share(k).start())
    out_ref[...] = read(adj, everything)

    def drain(r, c):
        for k in range(4):
            speed_copy(r, k).wait_send()
            later_copy(r, k).wait_send()
            solved_copy(r, k).wait_send()
            corner_copy(r, k).wait_send()
        return c

    lax.fori_loop(0, steps // 2, drain, 0)
    pltpu.make_async_copy(got, got, st_sem).wait()
    pltpu.make_async_copy(got, got, rt_sem).wait()
    summed = part[...] + jnp.sum(got[...], axis=0)
    grad_ref[...] = jnp.where(mine[...] > 0.0, summed, 0.0)[:, :turbines].reshape(grad_ref.shape)


def hand_over(parts, chunk, final_in, grad_in, final_out, grad_out, sem):
    moves = [pltpu.make_async_copy(grad_in, grad_out, sem.at[parts])]
    for k in range(parts):
        rows = pl.ds(k * chunk, chunk)
        moves.append(pltpu.make_async_copy(final_in.at[rows], final_out.at[rows], sem.at[k]))
    for move in moves:
        move.start()
    for move in moves:
        move.wait()


def body(sizes, adjoint_init, saved_states, step_index, vertical_inverse, disk_filter,
         pair_turbine, pair_tile, turbine_owner):
    ngx, ngy = sizes
    comps, sx, sy, levels = adjoint_init.shape
    saved = saved_states.shape[0]
    steps = step_index.shape[0]
    slots, points, cells = disk_filter.shape[2:]
    turbines = turbine_owner.shape[0]
    rows = comps * sx * sy
    lanes = -(-turbines // 128) * 128
    strip = comps * max(sx, sy) * levels // 128
    halves = levels // 128
    rounds = steps // 2
    count = ngx * ngy
    assert steps % 2 == 0 and sx == sy
    dims = (ngx, ngy, comps, sx, sy, steps, slots, points, turbines)
    anywhere = pl.BlockSpec(memory_space=pl.ANY)
    halo = lambda rows: pltpu.VMEM((rounds, 4, rows, 128), BF16)
    dma = pltpu.SemaphoreType.DMA
    final, grad = pl.pallas_call(
        functools.partial(kernel, dims),
        out_shape=(
            pltpu.VMEM((rows, levels), F32),
            pltpu.VMEM((1, 1, turbines), F32),
        ),
        in_specs=[pl.BlockSpec(memory_space=pltpu.HBM)] * 8,
        out_specs=(pl.BlockSpec(memory_space=pltpu.VMEM),) * 2,
        scratch_shapes=[
            pltpu.VMEM((halves, rows, 128), F32),
            pltpu.VMEM((saved, rows, levels), BF16),
            pltpu.SMEM(step_index.shape, jnp.int32),
            pltpu.VMEM((levels, levels), F32),
            pltpu.VMEM((slots * points, cells), BF16),
            pltpu.SMEM(pair_turbine.shape, jnp.int32),
            pltpu.SMEM(pair_tile.shape, jnp.int32),
            pltpu.SMEM(turbine_owner.shape, jnp.int32),
            pltpu.VMEM((levels, levels), BF16),
            pltpu.VMEM((levels, levels), BF16),
            pltpu.VMEM((halves, rows, 128), F32),
            pltpu.VMEM((steps, halves, rows, 128), F32),
            pltpu.VMEM((2, sx * sy, levels), BF16),
            pltpu.VMEM((2 * slots, sx * sy), BF16),
            pltpu.VMEM((slots, lanes), F32),
            pltpu.VMEM((1, lanes), F32),
            pltpu.VMEM((2, slots, slots * points), F32),
            pltpu.VMEM((slots, slots * points), F32),
            halo(2 * strip), halo(2 * strip), halo(strip), halo(strip), halo(2 * strip), halo(2 * strip),
            halo(8 * halves), halo(8 * halves),
            pltpu.VMEM((1, lanes), F32),
            pltpu.VMEM((count - 1, 1, lanes), F32),
            dma((7 + halves,)),
            *[dma((rounds, 4))] * 8,
            dma, dma,
        ],
        compiler_params=pltpu.CompilerParams(
            collective_id=0, has_side_effects=True, vmem_limit_bytes=60 * 1024 * 1024
        ),
        name="sweep",
    )(
        adjoint_init.reshape(rows, levels),
        saved_states.reshape(saved, rows, levels),
        step_index,
        vertical_inverse,
        disk_filter.reshape(slots * points, cells),
        pair_turbine,
        pair_tile,
        turbine_owner,
    )
    chunk = rows // comps
    final, grad = pl.pallas_call(
        functools.partial(hand_over, comps, chunk),
        out_shape=(
            jax.ShapeDtypeStruct((rows, levels), F32),
            jax.ShapeDtypeStruct((1, 1, turbines), F32),
        ),
        in_specs=[anywhere] * 2,
        out_specs=(anywhere, anywhere),
        scratch_shapes=[dma((comps + 1,))],
        compiler_params=pltpu.CompilerParams(vmem_limit_bytes=1024 * 1024),
        name="hand_over",
    )(final, grad)
    return final.reshape(adjoint_init.shape), grad


def solution(mesh):
    placed = (
        P(None, "gx", "gy", None),
        P(None, None, "gx", "gy", None),
        P(),
        P(),
        P("gx", "gy", None, None, None),
        P("gx", "gy", None),
        P("gx", "gy", None),
        P(),
    )
    return jax.shard_map(
        functools.partial(body, (mesh.shape["gx"], mesh.shape["gy"])),
        mesh=mesh,
        in_specs=placed,
        out_specs=(P(None, "gx", "gy", None), P("gx", "gy", None)),
        check_vma=False,
    )
```
